256 devices in a mesh: gx: 32 (over x, z), gy: 8 (over y, core).
Axes of the slice: x: 4, y: 4, z: 8, core: 2. Of those that a mesh axis runs over, the one named last changes fastest.
Arguments:
- displacement: float32 [3, 256, 128, 128], P(None, 'gx', 'gy'), may hold values from -6 to 6
- velocity: float32 [3, 256, 128, 128], P(None, 'gx', 'gy'), may hold values from -3 to 3
- plastic: float32 [30, 256, 128, 128], P(None, 'gx', 'gy'), may hold values from -1.2 to 1.2
- lumped_mass: float32 [256, 128, 128], P('gx', 'gy'), may hold values from 1 to 4
- material: int32 [256, 128, 128], P('gx', 'gy'), may hold values from 0 to 7
- moduli: float32 [8, 6], replicated, may hold values from 0.05 to 0.4
- yield_radii: float32 [8, 5], replicated, may hold values from 0.02 to 0.6
- history: float32 [1024, 21, 3072], P('gx', None, 'gy'), may hold values from -6 to 6
- drm_coef: float32 [1024, 2, 3072], P('gx', None, 'gy'), may hold values from 0.3 to 3
- layer_nodes: int32 [32, 98304], P('gx', 'gy'), may hold values from 0 to 16384, as said below
Outputs:
- final_displacement: float32 [3, 256, 128, 128], P(None, 'gx', 'gy')
- final_plastic: float32 [30, 256, 128, 128], P(None, 'gx', 'gy')
The draws below stay inside these ranges and needn't reach their ends.
Inputs may be any that keep to these rules, and one draw needn't show every extreme that they name: `layer_nodes`: entries are flat indices over (8, 16, 128) of a block's nodes, or 16384 for an empty slot; live entries of one block are distinct; the blocks at both ends along gx have all 12288 slots live, the others a quarter to a half of them.
All inputs are finite; a program needn't handle non-finite values.
Results may differ from the reference program's by a relative error of at most 0.0003.
Values sent between devices are 32-bit elements; how exact they have to be, the bound alone decides.
A program may use at most 128 MiB of HBM per device.

```python
import math
import jax
import jax.numpy as jnp
from jax import lax

EX = 8
EY = 16
NZ = 128
STEPS = 5
HS = 7
NSURF = 5
NMAT = 8
L_DEV = 12288
LPIECE = 384
NX = 256
NY = 128
READROWS = 1024
N_GX = 32
N_GY = 8


def draw_layer_nodes(key, part):
    node_count = EX * EY * NZ
    owners = N_GX * N_GY
    owner_keys = jax.random.split(jax.random.fold_in(key, 17), owners)

    def draw_owner(owner_key, owner_index):
        key_ids, key_count, key_rank = jax.random.split(owner_key, 3)
        node_ids = jax.random.permutation(key_ids, node_count)[:L_DEV].astype(jnp.int32)
        slab_index = owner_index // N_GY
        live_count = jax.random.randint(key_count, (), L_DEV // 4, L_DEV // 2 + 1)
        end_slab = (slab_index == 0) | (slab_index == N_GX - 1)
        live_count = jnp.where(end_slab, L_DEV, live_count)
        live_rank = jax.random.permutation(key_rank, L_DEV)
        return jnp.where(live_rank < live_count, node_ids, node_count).astype(jnp.int32)
    node_lists = jax.vmap(draw_owner)(owner_keys, jnp.arange(owners, dtype=jnp.int32))
    return node_lists.reshape(N_GX, N_GY * L_DEV)


def touch_ends(result, own_key, least, largest):
    longest = result.shape.index(max(result.shape))
    spots = []
    for shift in (0, 1):
        where = [jax.random.randint(jax.random.fold_in(own_key, axis), (), 0, length) for axis, length in enumerate(result.shape)]
        where[longest] = (where[longest] + shift) % result.shape[longest]
        spots.append(tuple(where))
    return result.at[spots[0]].set(least).at[spots[1]].set(largest)


def steps_of(rng, dims, shards, least, largest):
    factor_of = 1.0
    for dim, shards_of in shards:
        heights = jax.random.uniform(jax.random.fold_in(jax.random.fold_in(rng, 6), dim), (shards_of,), jnp.float32, least / len(shards), largest / len(shards))
        factor_of = factor_of * jnp.repeat(jnp.exp(heights), dims[dim] // shards_of).reshape((-1,) + (1,) * (len(dims) - 1 - dim))
    return factor_of


def noise(key, shape, scale, reach, cuts=(), kind=jnp.bfloat16):
    gain = steps_of(key, shape, cuts, -0.22, 0.18) if cuts else 1.0
    values = jax.random.normal(key, shape, jnp.float32) * scale * gain
    return jnp.minimum(jnp.maximum(values, -reach), reach).astype(kind)


def setup_inputs(seed: int = 0) -> dict:
    keys = jax.random.split(jax.random.key(seed), 11)
    return {
        "displacement": noise(keys[0], (3, NX, NY, NZ), 1.0, 6.0, ((1, 32), (2, 8)), jnp.float32),
        "velocity": noise(keys[1], (3, NX, NY, NZ), 0.5, 3.0, ((1, 32), (2, 8)), jnp.float32),
        "plastic": noise(keys[2], (6 * NSURF, NX, NY, NZ), 0.2, 1.2, ((1, 32), (2, 8)), jnp.float32),
        "lumped_mass": jnp.clip(jnp.exp(math.log(4.0) - 1.3862944 * jax.random.uniform(keys[3], (NX, NY, NZ), jnp.float32) ** steps_of(keys[3], (NX, NY, NZ), ((0, 32), (1, 8)), -0.2, 0.2)), 1.0, 4.0),
        "material": touch_ends(jax.random.randint(keys[4], (NX, NY, NZ), 0, NMAT), jax.random.fold_in(keys[4], 1), 0, NMAT - 1).astype(jnp.int32),
        "moduli": jnp.clip(jnp.exp(jax.random.uniform(keys[5], (NMAT, NSURF + 1), jnp.float32, math.log(0.05), math.log(0.4))), 0.05, 0.4),
        "yield_radii": jnp.clip(jnp.exp(jax.random.uniform(keys[6], (NMAT, NSURF), jnp.float32, math.log(0.02), math.log(0.6))), 0.02, 0.6),
        "history": noise(keys[7], (READROWS, 3 * HS, N_GY * LPIECE), 1.0, 6.0, ((0, 32), (2, 8)), jnp.float32),
        "drm_coef": jnp.clip(jnp.exp(math.log(3.0) - 2.3025851 * jax.random.uniform(keys[8], (READROWS, 2, N_GY * LPIECE), jnp.float32) ** steps_of(keys[8], (READROWS, 2, N_GY * LPIECE), ((0, 32), (2, 8)), -0.2, 0.2)), 0.3, 3.0),
        "layer_nodes": draw_layer_nodes(jax.random.fold_in(keys[10], 71), 0),
    }


time_step = 0.7

def corner(extended, near_x, near_y, near_z):
    return extended[:, near_x:near_x + extended.shape[1] - 1, near_y:near_y + extended.shape[2] - 1, near_z:near_z + extended.shape[3] - 1]

def material_props(material, moduli, yield_radii):
    soil_table = jnp.concatenate([moduli, yield_radii], axis=1)
    levels = jnp.arange(soil_table.shape[0], dtype=jnp.int32)
    onehot = (material[None] == levels[:, None, None, None]).astype(jnp.float32)
    return jnp.einsum('mxyz,mp->pxyz', onehot, soil_table, precision=lax.Precision.HIGHEST)

def drm_force(before, middle, after, coef_mass, coef_stiff):
    return coef_mass * (after - 2.0 * middle + before) + coef_stiff * middle

def element_forces(extended, plastic, material_data):
    grad_x = 0.0
    grad_y = 0.0
    grad_z = 0.0
    for near_y in (0, 1):
        for near_z in (0, 1):
            grad_x = grad_x + corner(extended, 1, near_y, near_z) - corner(extended, 0, near_y, near_z)
    for near_x in (0, 1):
        for near_z in (0, 1):
            grad_y = grad_y + corner(extended, near_x, 1, near_z) - corner(extended, near_x, 0, near_z)
    for near_x in (0, 1):
        for near_y in (0, 1):
            grad_z = grad_z + corner(extended, near_x, near_y, 1) - corner(extended, near_x, near_y, 0)
    grad_x = 0.25 * grad_x
    grad_y = 0.25 * grad_y
    grad_z = 0.25 * grad_z
    strain_xx = grad_x[0]
    strain_yy = grad_y[1]
    strain_zz = grad_z[2]
    strain_xy = 0.5 * (grad_y[0] + grad_x[1])
    strain_yz = 0.5 * (grad_z[1] + grad_y[2])
    strain_zx = 0.5 * (grad_x[2] + grad_z[0])
    volume_strain = strain_xx + strain_yy + strain_zz
    mean_strain = volume_strain / 3.0
    deviator = [strain_xx - mean_strain, strain_yy - mean_strain, strain_zz - mean_strain, strain_xy, strain_yz, strain_zx]
    surfaces = (material_data.shape[0] - 1) // 2
    deviator_sum = [jnp.zeros_like(strain_xx) for comp in range(6)]
    new_plastic = []
    for surface in range(surfaces):
        shear_mod = material_data[1 + surface]
        radius = material_data[1 + surfaces + surface]
        trial = [2.0 * shear_mod * (deviator[comp] - plastic[6 * surface + comp]) for comp in range(6)]
        sq_norm = trial[0] * trial[0] + trial[1] * trial[1] + trial[2] * trial[2] + 2.0 * (trial[3] * trial[3] + trial[4] * trial[4] + trial[5] * trial[5])
        radius_sq = radius * radius
        factor = jnp.sqrt(radius_sq / jnp.maximum(sq_norm, radius_sq))
        for comp in range(6):
            stress_part = factor * trial[comp]
            new_plastic.append(deviator[comp] - stress_part / (2.0 * shear_mod))
            deviator_sum[comp] = deviator_sum[comp] + stress_part
    bulk_mod = material_data[0]
    pressure = bulk_mod * volume_strain
    stress_xx = deviator_sum[0] + pressure
    stress_yy = deviator_sum[1] + pressure
    stress_zz = deviator_sum[2] + pressure
    stress_xy = deviator_sum[3]
    stress_yz = deviator_sum[4]
    stress_zx = deviator_sum[5]
    column_x = 0.25 * jnp.stack([stress_xx, stress_xy, stress_zx])
    column_y = 0.25 * jnp.stack([stress_xy, stress_yy, stress_yz])
    column_z = 0.25 * jnp.stack([stress_zx, stress_yz, stress_zz])
    force_ext = 0.0
    for near_x in (0, 1):
        for near_y in (0, 1):
            for near_z in (0, 1):
                corner_force = (2 * near_x - 1) * column_x + (2 * near_y - 1) * column_y + (2 * near_z - 1) * column_z
                force_ext = force_ext + jnp.pad(corner_force, ((0, 0), (near_x, 1 - near_x), (near_y, 1 - near_y), (near_z, 1 - near_z)))
    return (force_ext, jnp.stack(new_plastic))

def reference(displacement, velocity, plastic, lumped_mass, material, moduli, yield_radii, history, drm_coef, layer_nodes):
    material_data = material_props(material, moduli, yield_radii)
    levels = history.reshape(N_GX, N_GX, 3, HS, N_GY, LPIECE)
    coefs = drm_coef.reshape(N_GX, N_GX, 2, N_GY, LPIECE)
    coef_mass = coefs[:, :, 0][:, :, None]
    coef_stiff = coefs[:, :, 1][:, :, None]
    node_count = EX * EY * NZ
    node_lists = layer_nodes.reshape(N_GX, N_GY, L_DEV)
    local_x = node_lists // (EY * NZ)
    local_y = node_lists // NZ % EY
    local_z = node_lists % NZ
    slab_index = jnp.arange(N_GX, dtype=jnp.int32)[:, None, None]
    column_index = jnp.arange(N_GY, dtype=jnp.int32)[None, :, None]
    flat_index = ((slab_index * EX + local_x) * NY + column_index * EY + local_y) * NZ + local_z
    flat_index = jnp.where(node_lists < node_count, flat_index, NX * NY * NZ).astype(jnp.int32).reshape(-1)
    previous = displacement - time_step * velocity
    current = displacement
    for step_index in range(STEPS):
        values = drm_force(levels[:, :, :, step_index], levels[:, :, :, step_index + 1], levels[:, :, :, step_index + 2], coef_mass, coef_stiff)
        values = jnp.transpose(values, (2, 1, 3, 0, 4)).reshape(3, -1)
        drm_nodes = jnp.zeros((3, NX * NY * NZ), jnp.float32).at[:, flat_index].add(values, mode='drop').reshape(3, NX, NY, NZ)
        extended = jnp.pad(current, ((0, 0), (0, 1), (0, 1), (0, 1)))
        force_ext, plastic = element_forces(extended, plastic, material_data)
        internal = force_ext[:, :NX, :NY, :NZ]
        upcoming = 2.0 * current - previous + time_step * time_step * (drm_nodes - internal) / lumped_mass[None]
        previous = current
        current = upcoming
    return (current, plastic)
```

```python
import functools

import jax
import jax.numpy as jnp
from jax import lax
from jax.experimental import pallas as pl
from jax.experimental.pallas import tpu as pltpu
from jax.sharding import PartitionSpec as P

STEPS = 5
SURF = 5
TIME_STEP = 0.7
EX = 8
EY = 16
NZ = 128
PIECE = 384
MESH = pl.DeviceIdType.MESH
F32 = jnp.float32
BF16 = jnp.bfloat16


def lane_next(v):
    lane = lax.broadcasted_iota(jnp.int32, v.shape, 1)
    return jnp.where(lane < NZ - 1, pltpu.roll(v, NZ - 1, 1), 0.0)


def lane_before(v):
    lane = lax.broadcasted_iota(jnp.int32, v.shape, 1)
    return jnp.where(lane > 0, pltpu.roll(v, 1, 1), 0.0)


def strains(near, far):
    ss, ds, sd = [], [], []
    for c in range(3):
        s0, s1 = near[c][0] + near[c][1], far[c][0] + far[c][1]
        d0, d1 = near[c][1] - near[c][0], far[c][1] - far[c][0]
        ss.append(s0 + s1)
        ds.append(s1 - s0)
        sd.append(d0 + d1)

    def both(v):
        return v + lane_next(v)

    xx = 0.25 * both(ds[0])
    yy = 0.25 * both(sd[1])
    zz = 0.25 * (lane_next(ss[2]) - ss[2])
    xy = 0.125 * both(sd[0] + ds[1])
    yz = 0.125 * (lane_next(ss[1] + sd[2]) + (sd[2] - ss[1]))
    zx = 0.125 * (lane_next(ss[0] + ds[2]) + (ds[2] - ss[0]))
    trace = xx + yy + zz
    mean = trace * (1.0 / 3.0)
    return trace, [xx - mean, yy - mean, zz - mean, xy, yz, zx]


def stresses(trace, dev, read_plastic, write_plastic, read_prop):
    total = [None] * 6
    for s in range(SURF):
        shear2 = read_prop(1 + s)
        ratio = read_prop(1 + SURF + s)
        diff = [dev[k] - read_plastic(6 * s + k) for k in range(6)]
        w = diff[0] * diff[0] + diff[1] * diff[1] + diff[2] * diff[2]
        w = w + 2.0 * (diff[3] * diff[3] + diff[4] * diff[4] + diff[5] * diff[5])
        factor = ratio * lax.rsqrt(jnp.maximum(w, ratio * ratio))
        for k in range(6):
            kept = factor * diff[k]
            write_plastic(6 * s + k, dev[k] - kept)
            part = shear2 * kept
            total[k] = part if total[k] is None else total[k] + part
    pressure = read_prop(0) * trace
    return [total[k] + pressure if k < 3 else total[k] for k in range(6)]


def properties(mat, moduli, radii):
    def pick(table, column):
        value = jnp.full(mat.shape, table[0, column], F32)
        for m in range(1, 8):
            value = jnp.where(mat == float(m), table[m, column], value)
        return value

    shear2 = [2.0 * pick(moduli, 1 + s) for s in range(SURF)]
    ratio = [pick(radii, s) / shear2[s] for s in range(SURF)]
    return [pick(moduli, 0)] + shear2 + ratio


def kernel(
    nx, ny,
    disp, velo, plas, mass, mate, moduli, radii, hist, coef, nodes,
    out_disp, out_plas,
    U, V, W, YH, T, CS, CR, PL, PYS, PY, PCS, PCR, PR, PRY, SIG,
    FS, FR, H, B, A, ACC, WM, hv, cv, nv, velv, massv, matev,
    lsem, osem, a_send, a_recv, h_send, h_recv, p_send, p_recv,
):
    gx = lax.axis_index("gx")
    gy = lax.axis_index("gy")
    xn, xp = lax.rem(gx + 1, nx), lax.rem(gx + nx - 1, nx)
    yn, yp = lax.rem(gy + 1, ny), lax.rem(gy + ny - 1, ny)

    barrier = pltpu.get_barrier_semaphore()

    def greet(k, carry):
        pl.semaphore_signal(
            barrier, inc=1, device_id=(lax.rem(gx + k, nx), gy), device_id_type=MESH
        )
        return carry

    lax.fori_loop(1, nx, greet, 0)
    for place in ((gx, yn), (gx, yp), (xn, yn), (xn, yp), (xp, yn), (xp, yp)):
        pl.semaphore_signal(barrier, inc=1, device_id=place, device_id_type=MESH)

    loads = [
        pltpu.make_async_copy(src, dst, lsem.at[i])
        for i, (src, dst) in enumerate(
            (
                (hist, hv),
                (coef, cv),
                (plas, PL.at[pl.ds(0, 6 * SURF), pl.ds(1, EX)]),
                (disp, U.at[1, :, pl.ds(1, EX), pl.ds(0, EY)]),
                (mate, matev),
                (nodes, nv),
                (velo, velv),
                (mass, massv),
            )
        )
    ]
    for load in loads:
        load.start()

    loads[0].wait()
    loads[1].wait()

    def make_forces(a, carry):
        h = [hv[a, pl.ds(l, 19), :] for l in range(3)]
        force = cv[a, 0:1, :] * (h[2] - 2.0 * h[1] + h[0]) + cv[a, 1:2, :] * h[1]
        for n in range(STEPS):
            for c in range(3):
                FS[n, a, :, c * PIECE : (c + 1) * PIECE] = force[c * 7 + n : c * 7 + n + 1, :]
        return carry

    lax.fori_loop(0, nx, make_forces, 0)

    def own_forces(n, carry):
        FR[n, gx] = FS[n, gx]
        return carry

    lax.fori_loop(0, STEPS, own_forces, 0)

    loads[3].wait()

    def pack_rows(x, carry):
        for c in range(3):
            V[0, c, pl.ds(8 + x, 1), :] = U[1, c, x + 1, 0:1, :]
            YH[0, c, pl.ds(x, 1), :] = U[1, c, x + 1, EY - 1 : EY, :]
        return carry

    lax.fori_loop(0, EX, pack_rows, 0)

    def pack_corners(n):
        CS[n, 0] = V[n, :, 8:9, :]
        CS[n, 1] = YH[n, :, 0:1, :]
        CS[n, 2] = V[n, :, 15:16, :]
        CS[n, 3] = YH[n, :, 7:8, :]

    pack_corners(0)

    loads[4].wait()
    PL[6 * SURF, 1 : EX + 1] = matev[...].astype(F32)
    loads[2].wait()

    def pack_plastic(k, carry):
        for x in range(EX):
            PYS[k, x : x + 1, :] = PL[k, x + 1, EY - 1 : EY, :]
        PCS[k] = PYS[k, EX - 1 : EX, :]
        return carry

    lax.fori_loop(0, 6 * SURF + 1, pack_plastic, 0)

    pl.semaphore_wait(barrier, nx - 1 + 6)

    def remote(src, dst, send, recv, place):
        return pltpu.make_async_remote_copy(
            src_ref=src, dst_ref=dst, send_sem=send, recv_sem=recv, device_id=place,
            device_id_type=MESH,
        )

    def send_forces(n):
        def one(k, carry):
            to = lax.rem(gx + k, nx)
            remote(FS.at[n, to], FR.at[n, gx], a_send.at[n], a_recv.at[n], (to, gy)).start()
            return carry

        lax.fori_loop(1, nx, one, 0)

    def forces_done(n):
        some = FR.at[n, pl.ds(0, nx - 1)]
        return (
            pltpu.make_async_copy(some, some, a_send.at[n]),
            pltpu.make_async_copy(some, some, a_recv.at[n]),
        )

    def halo(n):
        own = pl.ds(0, EY)
        pairs = (
            (U.at[n + 1, :, 1, own], U.at[n + 1, :, EX + 1, own], (xp, gy)),
            (U.at[n + 1, :, EX, own], U.at[n + 1, :, 0, own], (xn, gy)),
            (V.at[n, :, pl.ds(8, 8)], T.at[n], (gx, yp)),
            (YH.at[n], W.at[n, :, pl.ds(8, 8)], (gx, yn)),
            (CS.at[n, 0], CR.at[n, 0], (xp, yp)),
            (CS.at[n, 1], CR.at[n, 1], (xp, yn)),
            (CS.at[n, 2], CR.at[n, 2], (xn, yp)),
            (CS.at[n, 3], CR.at[n, 3], (xn, yn)),
        )
        return [
            remote(src, dst, h_send.at[n, i], h_recv.at[n, i], place)
            for i, (src, dst, place) in enumerate(pairs)
        ]

    def plastic_halo():
        pairs = (
            (PL.at[:, EX], PL.at[:, 0], (xn, gy)),
            (PYS, PY.at[:, pl.ds(8, 8)], (gx, yn)),
            (PCS, PCR, (xn, yn)),
        )
        return [
            remote(src, dst, p_send.at[i], p_recv.at[i], place)
            for i, (src, dst, place) in enumerate(pairs)
        ]

    for copy in halo(0):
        copy.start()
    send_forces(0)
    for copy in plastic_halo():
        copy.start()
    send_forces(1)

    loads[5].wait()

    def one_hot(r, carry):
        v = nv[:, pl.ds(pl.multiple_of(r * PIECE, 128), PIECE)]
        high = (v // 2048) * 8 + (v // 128) % 8
        low = ((v // 1024) % 2) * 128 + v % 128
        rows = lax.broadcasted_iota(jnp.int32, (64, PIECE), 0)
        H[r] = jnp.where(rows == high, 1.0, 0.0).astype(BF16)
        rows = lax.broadcasted_iota(jnp.int32, (256, PIECE), 0)
        B[r] = jnp.where(rows == low, 1.0, 0.0).astype(BF16)
        return carry

    lax.fori_loop(0, nx, one_hot, 0)

    def own_props(x, carry):
        for k, value in enumerate(properties(PL[6 * SURF, x], moduli, radii)):
            PR[k, x] = value
        return carry

    lax.fori_loop(1, EX + 1, own_props, 0)

    for load in loads[6:]:
        load.wait()
    WM[...] = (TIME_STEP * TIME_STEP) / massv[...]
    U[0, :, 1 : EX + 1, 0:EY] = U[1, :, 1 : EX + 1, 0:EY] - TIME_STEP * velv[...]

    for copy in plastic_halo():
        copy.wait()
    PY[:, 7:8, :] = PCR[...]
    live_x = jnp.where(gx > 0, 1.0, 0.0).astype(F32)
    live_y = jnp.where(gy > 0, 1.0, 0.0).astype(F32)
    for k, value in enumerate(properties(PL[6 * SURF, 0], moduli, radii)):
        PR[k, 0] = value * live_x if k <= SURF else value
    row = lax.broadcasted_iota(jnp.int32, (16, NZ), 0)
    live = jnp.where(row <= 7, live_x * live_y, live_y)
    for k, value in enumerate(properties(PY[6 * SURF], moduli, radii)):
        PRY[k] = value * live if k <= SURF else value

    def scatter(n):
        ACC[...] = jnp.zeros_like(ACC)

        def pair(j, carry):
            for p in (0, 1):
                r = 2 * j + p
                v = jnp.broadcast_to(FR[n, r], (16, 3 * PIECE))
                head = v.astype(BF16)
                tail = (v - head.astype(F32)).astype(BF16)
                for g in range(4):
                    hot = H[r, g * 16 : (g + 1) * 16, :]
                    for i, part in enumerate((head, tail)):
                        for c in range(3):
                            top = (i * 3 + c) * 64 + g * 16
                            A[top : top + 16, p * PIECE : (p + 1) * PIECE] = (
                                hot * part[:, c * PIECE : (c + 1) * PIECE]
                            )
            both = jnp.concatenate([B[2 * j], B[2 * j + 1]], axis=1)
            ACC[...] += lax.dot_general(
                A[...], both, (((1,), (1,)), ((), ())), preferred_element_type=F32
            )
            return carry

        lax.fori_loop(0, nx // 2, pair, 0)

    def step(n, carry):
        for copy in forces_done(n):
            copy.wait()
        scatter(n)

        copies = halo(n)
        for copy in copies:
            copy.wait_recv()

        def unpack(x, inner):
            for c in range(3):
                U[n + 1, c, x + 1, EY : EY + 1, :] = T[n, c, pl.ds(x, 1), :]
            return inner

        lax.fori_loop(0, EX, unpack, 0)
        U[n + 1, :, EX + 1, EY : EY + 1, :] = CR[n, 0]
        W[n, :, 16:17, :] = CR[n, 1]
        U[n + 1, :, 0, EY : EY + 1, :] = CR[n, 2]
        W[n, :, 7:8, :] = CR[n, 3]

        @pl.when(gx == nx - 1)
        def _():
            U[n + 1, :, EX + 1] = jnp.zeros((3, 24, NZ), F32)
            W[n, :, 16:17, :] = jnp.zeros((3, 1, NZ), F32)

        @pl.when(gy == ny - 1)
        def _():
            U[n + 1, :, :, EY : EY + 8] = jnp.zeros((3, EX + 2, 8, NZ), F32)

        V[n, :, 7:8, :] = U[n + 1, :, 0, 0:1, :]
        V[n, :, 16:17, :] = U[n + 1, :, EX + 1, 0:1, :]

        for t in range(2):
            lo = pl.ds(t * 8, 8)
            up = pl.ds(t * 8 + 1, 8)
            near = [(W[n, c, lo, :], V[n, c, lo, :]) for c in range(3)]
            far = [(W[n, c, up, :], V[n, c, up, :]) for c in range(3)]
            trace, dev = strains(near, far)

            def write(k, value):
                PY[k, lo, :] = value

            sigma = stresses(trace, dev, lambda k: PY[k, lo, :], write, lambda k: PRY[k, lo, :])
            for k in range(6):
                if t == 0:
                    SIG[k, 0, 7:8, :] = sigma[k][7:8, :]
                else:
                    for x in range(EX):
                        SIG[k, x + 1, 7:8, :] = sigma[k][x : x + 1, :]

        def elements(x, inner):
            for t in range(2):
                lo = pl.ds(t * 8, 8)
                up = pl.ds(t * 8 + 1, 8)
                near = [(U[n + 1, c, x, lo, :], U[n + 1, c, x, up, :]) for c in range(3)]
                far = [(U[n + 1, c, x + 1, lo, :], U[n + 1, c, x + 1, up, :]) for c in range(3)]
                trace, dev = strains(near, far)

                def write(k, value):
                    PL[k, x, lo, :] = value

                sigma = stresses(
                    trace, dev, lambda k: PL[k, x, lo, :], write, lambda k: PR[k, x, lo, :]
                )
                for k in range(6):
                    SIG[k, x, t * 8 + 8 : t * 8 + 16, :] = sigma[k]
            return inner

        lax.fori_loop(0, EX + 1, elements, 0)

        def update(x, inner):
            for t in range(2):
                old = pl.ds(t * 8 + 7, 8)
                new = pl.ds(t * 8 + 8, 8)
                lo = pl.ds(t * 8, 8)
                minus, plus = {}, {}
                for k in range(6):
                    for rows in (0, 1):
                        at = new if rows else old
                        before, here = SIG[k, x, at, :], SIG[k, x + 1, at, :]
                        plus[k, rows] = before + here
                        if k in (0, 3, 5):
                            minus[k, rows] = before - here
                for c, (kx, ky, kz) in enumerate(((0, 3, 5), (3, 1, 4), (5, 4, 2))):
                    across = (minus[kx, 0] + plus[ky, 0]) + (minus[kx, 1] - plus[ky, 1])
                    down = plus[kz, 0] + plus[kz, 1]
                    inside = lane_before(across + down) + (across - down)
                    top = c * 64 + x * 8
                    lanes = slice(t * 128, (t + 1) * 128)
                    placed = ACC[pl.ds(top, 8), lanes] + ACC[pl.ds(192 + top, 8), lanes]
                    now = U[n + 1, c, x + 1, lo, :]
                    later = (
                        2.0 * now
                        - U[n, c, x + 1, lo, :]
                        + WM[x, lo, :] * (placed - 0.25 * inside)
                    )
                    U[n + 2, c, x + 1, lo, :] = later
                    if t == 0:
                        V[n + 1, c, pl.ds(8 + x, 1), :] = later[0:1, :]
                    else:
                        YH[n + 1, c, pl.ds(x, 1), :] = later[7:8, :]
            return inner

        lax.fori_loop(0, EX, update, 0)

        @pl.when(n < STEPS - 1)
        def _():
            pack_corners(n + 1)
            for copy in halo(n + 1):
                copy.start()

        @pl.when(n < STEPS - 2)
        def _():
            send_forces(n + 2)

        for copy in copies:
            copy.wait_send()
        return carry

    lax.fori_loop(0, STEPS, step, 0)
    outs = [
        pltpu.make_async_copy(
            U.at[STEPS + 1, :, pl.ds(1, EX), pl.ds(0, EY)], out_disp, osem.at[0]
        ),
        pltpu.make_async_copy(PL.at[pl.ds(0, 6 * SURF), pl.ds(1, EX)], out_plas, osem.at[1]),
    ]
    for out in outs:
        out.start()
    for out in outs:
        out.wait()


def per_device(nx, ny, *args):
    any_space = pl.BlockSpec(memory_space=pl.ANY)
    smem = pl.BlockSpec(memory_space=pltpu.SMEM)
    vmem = pltpu.VMEM
    dma = pltpu.SemaphoreType.DMA
    scratch = [
        vmem((STEPS + 2, 3, EX + 2, EY + 8, NZ), F32),
        vmem((STEPS + 1, 3, 24, NZ), F32),
        vmem((STEPS, 3, 24, NZ), F32),
        vmem((STEPS + 1, 3, 8, NZ), F32),
        vmem((STEPS, 3, 8, NZ), F32),
        vmem((STEPS, 4, 3, 1, NZ), F32),
        vmem((STEPS, 4, 3, 1, NZ), F32),
        vmem((6 * SURF + 1, EX + 1, EY, NZ), F32),
        vmem((6 * SURF + 1, EX, NZ), F32),
        vmem((6 * SURF + 1, 16, NZ), F32),
        vmem((6 * SURF + 1, 1, NZ), F32),
        vmem((6 * SURF + 1, 1, NZ), F32),
        vmem((1 + 2 * SURF, EX + 1, EY, NZ), F32),
        vmem((1 + 2 * SURF, 16, NZ), F32),
        vmem((6, EX + 1, EY + 8, NZ), F32),
        vmem((STEPS, nx, 1, 3 * PIECE), F32),
        vmem((STEPS, nx, 1, 3 * PIECE), F32),
        vmem((nx, 64, PIECE), BF16),
        vmem((nx, 256, PIECE), BF16),
        vmem((384, 2 * PIECE), BF16),
        vmem((384, 256), F32),
        vmem((EX, EY, NZ), F32),
        vmem((nx, 21, PIECE), F32),
        vmem((nx, 2, PIECE), F32),
        vmem((1, nx * PIECE), jnp.int32),
        vmem((3, EX, EY, NZ), F32),
        vmem((EX, EY, NZ), F32),
        vmem((EX, EY, NZ), jnp.int32),
        dma((8,)),
        dma((2,)),
        dma((STEPS,)),
        dma((STEPS,)),
        dma((STEPS, 8)),
        dma((STEPS, 8)),
        dma((3,)),
        dma((3,)),
    ]
    return pl.pallas_call(
        functools.partial(kernel, nx, ny),
        out_shape=(
            jax.ShapeDtypeStruct((3, EX, EY, NZ), F32),
            jax.ShapeDtypeStruct((6 * SURF, EX, EY, NZ), F32),
        ),
        in_specs=[any_space] * 5 + [smem] * 2 + [any_space] * 3,
        out_specs=(any_space, any_space),
        scratch_shapes=scratch,
        compiler_params=pltpu.CompilerParams(
            collective_id=0, has_side_effects=True, vmem_limit_bytes=48 * 1024 * 1024
        ),
        name="box_steps",
    )(*args)


def solution(mesh):
    return jax.shard_map(
        functools.partial(per_device, mesh.shape["gx"], mesh.shape["gy"]),
        mesh=mesh,
        in_specs=(
            P(None, "gx", "gy", None),
            P(None, "gx", "gy", None),
            P(None, "gx", "gy", None),
            P("gx", "gy", None),
            P("gx", "gy", None),
            P(),
            P(),
            P("gx", None, "gy"),
            P("gx", None, "gy"),
            P("gx", "gy"),
        ),
        out_specs=(P(None, "gx", "gy", None), P(None, "gx", "gy", None)),
        check_vma=False,
    )
```

```python
import functools

import jax
import jax.numpy as jnp
from jax import lax
from jax.experimental import pallas as pl
from jax.experimental.pallas import tpu as pltpu
from jax.sharding import PartitionSpec as P

STEPS = 5
SURF = 5
TIME_STEP = 0.7
EX = 8
EY = 16
NZ = 128
PIECE = 384
MESH = pl.DeviceIdType.MESH
F32 = jnp.float32
BF16 = jnp.bfloat16


def lane_next(v):
    lane = lax.broadcasted_iota(jnp.int32, v.shape, 1)
    return jnp.where(lane < NZ - 1, pltpu.roll(v, NZ - 1, 1), 0.0)


def lane_before(v):
    lane = lax.broadcasted_iota(jnp.int32, v.shape, 1)
    return jnp.where(lane > 0, pltpu.roll(v, 1, 1), 0.0)


def strains(near, far):
    ss, ds, sd = [], [], []
    for c in range(3):
        s0, s1 = near[c][0] + near[c][1], far[c][0] + far[c][1]
        d0, d1 = near[c][1] - near[c][0], far[c][1] - far[c][0]
        ss.append(s0 + s1)
        ds.append(s1 - s0)
        sd.append(d0 + d1)

    def both(v):
        return v + lane_next(v)

    xx = 0.25 * both(ds[0])
    yy = 0.25 * both(sd[1])
    zz = 0.25 * (lane_next(ss[2]) - ss[2])
    xy = 0.125 * both(sd[0] + ds[1])
    yz = 0.125 * (lane_next(ss[1] + sd[2]) + (sd[2] - ss[1]))
    zx = 0.125 * (lane_next(ss[0] + ds[2]) + (ds[2] - ss[0]))
    trace = xx + yy + zz
    mean = trace * (1.0 / 3.0)
    return trace, [xx - mean, yy - mean, zz - mean, xy, yz, zx]


def stresses(trace, dev, read_plastic, write_plastic, read_prop):
    total = [None] * 6
    for s in range(SURF):
        shear2 = read_prop(1 + s)
        ratio = read_prop(1 + SURF + s)
        diff = [dev[k] - read_plastic(6 * s + k) for k in range(6)]
        w = diff[0] * diff[0] + diff[1] * diff[1] + diff[2] * diff[2]
        w = w + 2.0 * (diff[3] * diff[3] + diff[4] * diff[4] + diff[5] * diff[5])
        factor = ratio * lax.rsqrt(jnp.maximum(w, ratio * ratio))
        for k in range(6):
            kept = factor * diff[k]
            write_plastic(6 * s + k, dev[k] - kept)
            part = shear2 * kept
            total[k] = part if total[k] is None else total[k] + part
    pressure = read_prop(0) * trace
    return [total[k] + pressure if k < 3 else total[k] for k in range(6)]


def properties(mat, moduli, radii):
    def pick(table, column):
        value = jnp.full(mat.shape, table[0, column], F32)
        for m in range(1, 8):
            value = jnp.where(mat == float(m), table[m, column], value)
        return value

    shear2 = [2.0 * pick(moduli, 1 + s) for s in range(SURF)]
    ratio = [pick(radii, s) / shear2[s] for s in range(SURF)]
    return [pick(moduli, 0)] + shear2 + ratio


def kernel(
    nx, ny,
    disp, velo, plas, mass, mate, moduli, radii, hist, coef, nodes,
    out_disp, out_plas,
    U, V, W, YH, T, CS, CR, PL, PYS, PY, PCS, PCR, PR, PRY, SIG,
    FS, FR, H, B, A, ACC, WM, hv, cv, ct, nv, velv, massv, matev,
    lsem, osem, a_send, a_recv, h_send, h_recv, p_send, p_recv,
):
    gx = lax.axis_index("gx")
    gy = lax.axis_index("gy")
    xn, xp = lax.rem(gx + 1, nx), lax.rem(gx + nx - 1, nx)
    yn, yp = lax.rem(gy + 1, ny), lax.rem(gy + ny - 1, ny)

    barrier = pltpu.get_barrier_semaphore()

    def greet(k, carry):
        pl.semaphore_signal(
            barrier, inc=1, device_id=(lax.rem(gx + k, nx), gy), device_id_type=MESH
        )
        return carry

    lax.fori_loop(1, nx, greet, 0)
    for place in ((gx, yn), (gx, yp), (xn, yn), (xn, yp), (xp, yn), (xp, yp)):
        pl.semaphore_signal(barrier, inc=1, device_id=place, device_id_type=MESH)

    loads = [
        pltpu.make_async_copy(src, dst, lsem.at[i])
        for i, (src, dst) in enumerate(
            (
                (hist, hv),
                (coef, cv),
                (plas, PL.at[pl.ds(0, 6 * SURF), pl.ds(1, EX)]),
                (disp, U.at[1, :, pl.ds(1, EX), pl.ds(0, EY)]),
                (mate, matev),
                (nodes, nv),
                (velo, velv),
                (mass, massv),
            )
        )
    ]
    for load in loads:
        load.start()

    loads[0].wait()
    loads[1].wait()

    def split_coef(a, carry):
        for j in range(2):
            ct[j, pl.ds(a, 1), :] = cv[a, j : j + 1, :]
        return carry

    lax.fori_loop(0, nx, split_coef, 0, unroll=4)

    def make_forces(g, carry):
        rows = pl.ds(pl.multiple_of(g * 8, 8), 8)
        cm, ck = ct[0, rows, :], ct[1, rows, :]
        for c in range(3):
            h = [hv[c * 7 + l, rows, :] for l in range(STEPS + 2)]
            for n in range(STEPS):
                force = cm * (h[n + 2] - 2.0 * h[n + 1] + h[n]) + ck * h[n + 1]
                for i in range(8):
                    FS[n, g * 8 + i, :, c * PIECE : (c + 1) * PIECE] = force[i : i + 1, :]
        return carry

    lax.fori_loop(0, nx // 8, make_forces, 0)

    def own_forces(n, carry):
        FR[n, gx] = FS[n, gx]
        return carry

    lax.fori_loop(0, STEPS, own_forces, 0)

    loads[3].wait()

    def pack_rows(x, carry):
        for c in range(3):
            V[0, c, pl.ds(8 + x, 1), :] = U[1, c, x + 1, 0:1, :]
            YH[0, c, pl.ds(x, 1), :] = U[1, c, x + 1, EY - 1 : EY, :]
        return carry

    lax.fori_loop(0, EX, pack_rows, 0)

    def pack_corners(n):
        CS[n, 0] = V[n, :, 8:9, :]
        CS[n, 1] = YH[n, :, 0:1, :]
        CS[n, 2] = V[n, :, 15:16, :]
        CS[n, 3] = YH[n, :, 7:8, :]

    pack_corners(0)

    loads[4].wait()
    PL[6 * SURF, 1 : EX + 1] = matev[...].astype(F32)
    loads[2].wait()

    def pack_plastic(k, carry):
        for x in range(EX):
            PYS[k, x : x + 1, :] = PL[k, x + 1, EY - 1 : EY, :]
        PCS[k] = PYS[k, EX - 1 : EX, :]
        return carry

    lax.fori_loop(0, 6 * SURF + 1, pack_plastic, 0)

    pl.semaphore_wait(barrier, nx - 1 + 6)

    def remote(src, dst, send, recv, place):
        return pltpu.make_async_remote_copy(
            src_ref=src, dst_ref=dst, send_sem=send, recv_sem=recv, device_id=place,
            device_id_type=MESH,
        )

    def send_forces(n):
        def one(k, carry):
            to = lax.rem(gx + k, nx)
            remote(FS.at[n, to], FR.at[n, gx], a_send.at[n], a_recv.at[n], (to, gy)).start()
            return carry

        lax.fori_loop(1, nx, one, 0)

    def forces_done(n):
        some = FR.at[n, pl.ds(0, nx - 1)]
        return (
            pltpu.make_async_copy(some, some, a_send.at[n]),
            pltpu.make_async_copy(some, some, a_recv.at[n]),
        )

    def halo(n):
        own = pl.ds(0, EY)
        pairs = (
            (U.at[n + 1, :, 1, own], U.at[n + 1, :, EX + 1, own], (xp, gy)),
            (U.at[n + 1, :, EX, own], U.at[n + 1, :, 0, own], (xn, gy)),
            (V.at[n, :, pl.ds(8, 8)], T.at[n], (gx, yp)),
            (YH.at[n], W.at[n, :, pl.ds(8, 8)], (gx, yn)),
            (CS.at[n, 0], CR.at[n, 0], (xp, yp)),
            (CS.at[n, 1], CR.at[n, 1], (xp, yn)),
            (CS.at[n, 2], CR.at[n, 2], (xn, yp)),
            (CS.at[n, 3], CR.at[n, 3], (xn, yn)),
        )
        return [
            remote(src, dst, h_send.at[n, i], h_recv.at[n, i], place)
            for i, (src, dst, place) in enumerate(pairs)
        ]

    def plastic_halo():
        pairs = (
            (PL.at[:, EX], PL.at[:, 0], (xn, gy)),
            (PYS, PY.at[:, pl.ds(8, 8)], (gx, yn)),
            (PCS, PCR, (xn, yn)),
        )
        return [
            remote(src, dst, p_send.at[i], p_recv.at[i], place)
            for i, (src, dst, place) in enumerate(pairs)
        ]

    for copy in halo(0):
        copy.start()
    send_forces(0)
    for copy in plastic_halo():
        copy.start()
    send_forces(1)

    loads[5].wait()

    def one_hot(r, carry):
        v = nv[:, pl.ds(pl.multiple_of(r * PIECE, 128), PIECE)]
        high = (v // 2048) * 8 + (v // 128) % 8
        low = ((v // 1024) % 2) * 128 + v % 128
        rows = lax.broadcasted_iota(jnp.int32, (64, PIECE), 0)
        H[r] = jnp.where(rows == high, 1.0, 0.0).astype(BF16)
        rows = lax.broadcasted_iota(jnp.int32, (256, PIECE), 0)
        at = pl.ds(pl.multiple_of(r * PIECE, 128), PIECE)
        B[:, at] = jnp.where(rows == low, 1.0, 0.0).astype(BF16)
        return carry

    lax.fori_loop(0, nx, one_hot, 0)

    def own_props(x, carry):
        for k, value in enumerate(properties(PL[6 * SURF, x], moduli, radii)):
            PR[k, x] = value
        return carry

    lax.fori_loop(1, EX + 1, own_props, 0)

    for load in loads[6:]:
        load.wait()
    WM[...] = (TIME_STEP * TIME_STEP) / massv[...]
    U[0, :, 1 : EX + 1, 0:EY] = U[1, :, 1 : EX + 1, 0:EY] - TIME_STEP * velv[...]

    def scatter(n):
        def spread(r, carry):
            v = jnp.broadcast_to(FR[n, r], (16, 3 * PIECE))
            head = v.astype(BF16)
            tail = (v - head.astype(F32)).astype(BF16)
            at = pl.ds(pl.multiple_of(r * PIECE, 128), PIECE)
            for g in range(4):
                hot = H[r, g * 16 : (g + 1) * 16, :]
                for i, part in enumerate((head, tail)):
                    for c in range(3):
                        top = (i * 3 + c) * 64 + g * 16
                        A[top : top + 16, at] = hot * part[:, c * PIECE : (c + 1) * PIECE]
            return carry

        lax.fori_loop(0, nx, spread, 0, unroll=nx)
        ACC[...] = lax.dot_general(
            A[...], B[...], (((1,), (1,)), ((), ())), preferred_element_type=F32
        )

    outs = [
        pltpu.make_async_copy(
            U.at[STEPS + 1, :, pl.ds(1, EX), pl.ds(0, EY)], out_disp, osem.at[0]
        ),
        pltpu.make_async_copy(PL.at[pl.ds(0, 6 * SURF), pl.ds(1, EX)], out_plas, osem.at[1]),
    ]

    def step(n, carry):
        for copy in forces_done(n):
            copy.wait()
        scatter(n)

        @pl.when(n == 0)
        def _():
            for copy in plastic_halo():
                copy.wait()
            PY[:, 7:8, :] = PCR[...]
            live_x = jnp.where(gx > 0, 1.0, 0.0).astype(F32)
            live_y = jnp.where(gy > 0, 1.0, 0.0).astype(F32)
            for k, value in enumerate(properties(PL[6 * SURF, 0], moduli, radii)):
                PR[k, 0] = value * live_x if k <= SURF else value
            row = lax.broadcasted_iota(jnp.int32, (16, NZ), 0)
            live = jnp.where(row <= 7, live_x * live_y, live_y)
            for k, value in enumerate(properties(PY[6 * SURF], moduli, radii)):
                PRY[k] = value * live if k <= SURF else value

        copies = halo(n)
        for copy in copies:
            copy.wait_recv()

        def unpack(x, inner):
            for c in range(3):
                U[n + 1, c, x + 1, EY : EY + 1, :] = T[n, c, pl.ds(x, 1), :]
            return inner

        lax.fori_loop(0, EX, unpack, 0)
        U[n + 1, :, EX + 1, EY : EY + 1, :] = CR[n, 0]
        W[n, :, 16:17, :] = CR[n, 1]
        U[n + 1, :, 0, EY : EY + 1, :] = CR[n, 2]
        W[n, :, 7:8, :] = CR[n, 3]

        @pl.when(gx == nx - 1)
        def _():
            U[n + 1, :, EX + 1] = jnp.zeros((3, 24, NZ), F32)
            W[n, :, 16:17, :] = jnp.zeros((3, 1, NZ), F32)

        @pl.when(gy == ny - 1)
        def _():
            U[n + 1, :, :, EY : EY + 8] = jnp.zeros((3, EX + 2, 8, NZ), F32)

        V[n, :, 7:8, :] = U[n + 1, :, 0, 0:1, :]
        V[n, :, 16:17, :] = U[n + 1, :, EX + 1, 0:1, :]

        for t in range(2):
            lo = pl.ds(t * 8, 8)
            up = pl.ds(t * 8 + 1, 8)
            near = [(W[n, c, lo, :], V[n, c, lo, :]) for c in range(3)]
            far = [(W[n, c, up, :], V[n, c, up, :]) for c in range(3)]
            trace, dev = strains(near, far)

            def write(k, value):
                PY[k, lo, :] = value

            sigma = stresses(trace, dev, lambda k: PY[k, lo, :], write, lambda k: PRY[k, lo, :])
            for k in range(6):
                if t == 0:
                    SIG[k, 0, 7:8, :] = sigma[k][7:8, :]
                else:
                    for x in range(EX):
                        SIG[k, x + 1, 7:8, :] = sigma[k][x : x + 1, :]

        def elements(x, inner):
            for t in range(2):
                lo = pl.ds(t * 8, 8)
                up = pl.ds(t * 8 + 1, 8)
                near = [(U[n + 1, c, x, lo, :], U[n + 1, c, x, up, :]) for c in range(3)]
                far = [(U[n + 1, c, x + 1, lo, :], U[n + 1, c, x + 1, up, :]) for c in range(3)]
                trace, dev = strains(near, far)

                def write(k, value):
                    PL[k, x, lo, :] = value

                sigma = stresses(
                    trace, dev, lambda k: PL[k, x, lo, :], write, lambda k: PR[k, x, lo, :]
                )
                for k in range(6):
                    SIG[k, x, t * 8 + 8 : t * 8 + 16, :] = sigma[k]
            return inner

        lax.fori_loop(0, EX + 1, elements, 0, unroll=EX + 1)

        @pl.when(n == STEPS - 1)
        def _():
            outs[1].start()

        def update(x, inner):
            for t in range(2):
                old = pl.ds(t * 8 + 7, 8)
                new = pl.ds(t * 8 + 8, 8)
                lo = pl.ds(t * 8, 8)
                minus, plus = {}, {}
                for k in range(6):
                    for rows in (0, 1):
                        at = new if rows else old
                        before, here = SIG[k, x, at, :], SIG[k, x + 1, at, :]
                        plus[k, rows] = before + here
                        if k in (0, 3, 5):
                            minus[k, rows] = before - here
                for c, (kx, ky, kz) in enumerate(((0, 3, 5), (3, 1, 4), (5, 4, 2))):
                    across = (minus[kx, 0] + plus[ky, 0]) + (minus[kx, 1] - plus[ky, 1])
                    down = plus[kz, 0] + plus[kz, 1]
                    inside = lane_before(across + down) + (across - down)
                    top = c * 64 + x * 8
                    lanes = slice(t * 128, (t + 1) * 128)
                    placed = ACC[pl.ds(top, 8), lanes] + ACC[pl.ds(192 + top, 8), lanes]
                    now = U[n + 1, c, x + 1, lo, :]
                    later = (
                        2.0 * now
                        - U[n, c, x + 1, lo, :]
                        + WM[x, lo, :] * (placed - 0.25 * inside)
                    )
                    U[n + 2, c, x + 1, lo, :] = later
                    if t == 0:
                        V[n + 1, c, pl.ds(8 + x, 1), :] = later[0:1, :]
                    else:
                        YH[n + 1, c, pl.ds(x, 1), :] = later[7:8, :]
            return inner

        lax.fori_loop(0, EX, update, 0, unroll=EX)

        @pl.when(n < STEPS - 1)
        def _():
            pack_corners(n + 1)
            for copy in halo(n + 1):
                copy.start()

        @pl.when(n < STEPS - 2)
        def _():
            send_forces(n + 2)

        for copy in copies:
            copy.wait_send()
        return carry

    lax.fori_loop(0, STEPS, step, 0)
    outs[0].start()
    for out in outs:
        out.wait()


def per_device(nx, ny, *args):
    any_space = pl.BlockSpec(memory_space=pl.ANY)
    smem = pl.BlockSpec(memory_space=pltpu.SMEM)
    vmem = pltpu.VMEM
    dma = pltpu.SemaphoreType.DMA
    scratch = [
        vmem((STEPS + 2, 3, EX + 2, EY + 8, NZ), F32),
        vmem((STEPS + 1, 3, 24, NZ), F32),
        vmem((STEPS, 3, 24, NZ), F32),
        vmem((STEPS + 1, 3, 8, NZ), F32),
        vmem((STEPS, 3, 8, NZ), F32),
        vmem((STEPS, 4, 3, 1, NZ), F32),
        vmem((STEPS, 4, 3, 1, NZ), F32),
        vmem((6 * SURF + 1, EX + 1, EY, NZ), F32),
        vmem((6 * SURF + 1, EX, NZ), F32),
        vmem((6 * SURF + 1, 16, NZ), F32),
        vmem((6 * SURF + 1, 1, NZ), F32),
        vmem((6 * SURF + 1, 1, NZ), F32),
        vmem((1 + 2 * SURF, EX + 1, EY, NZ), F32),
        vmem((1 + 2 * SURF, 16, NZ), F32),
        vmem((6, EX + 1, EY + 8, NZ), F32),
        vmem((STEPS, nx, 1, 3 * PIECE), F32),
        vmem((STEPS, nx, 1, 3 * PIECE), F32),
        vmem((nx, 64, PIECE), BF16),
        vmem((256, nx * PIECE), BF16),
        vmem((384, nx * PIECE), BF16),
        vmem((384, 256), F32),
        vmem((EX, EY, NZ), F32),
        vmem((21, nx, PIECE), F32),
        vmem((nx, 2, PIECE), F32),
        vmem((2, nx, PIECE), F32),
        vmem((1, nx * PIECE), jnp.int32),
        vmem((3, EX, EY, NZ), F32),
        vmem((EX, EY, NZ), F32),
        vmem((EX, EY, NZ), jnp.int32),
        dma((8,)),
        dma((2,)),
        dma((STEPS,)),
        dma((STEPS,)),
        dma((STEPS, 8)),
        dma((STEPS, 8)),
        dma((3,)),
        dma((3,)),
    ]
    return pl.pallas_call(
        functools.partial(kernel, nx, ny),
        out_shape=(
            jax.ShapeDtypeStruct((3, EX, EY, NZ), F32),
            jax.ShapeDtypeStruct((6 * SURF, EX, EY, NZ), F32),
        ),
        in_specs=[any_space] * 5 + [smem] * 2 + [any_space] * 3,
        out_specs=(any_space, any_space),
        scratch_shapes=scratch,
        compiler_params=pltpu.CompilerParams(
            collective_id=0, has_side_effects=True, vmem_limit_bytes=60 * 1024 * 1024
        ),
        name="box_steps",
    )(*args[:7], jnp.transpose(args[7], (1, 0, 2)), *args[8:])


def solution(mesh):
    return jax.shard_map(
        functools.partial(per_device, mesh.shape["gx"], mesh.shape["gy"]),
        mesh=mesh,
        in_specs=(
            P(None, "gx", "gy", None),
            P(None, "gx", "gy", None),
            P(None, "gx", "gy", None),
            P("gx", "gy", None),
            P("gx", "gy", None),
            P(),
            P(),
            P("gx", None, "gy"),
            P("gx", None, "gy"),
            P("gx", "gy"),
        ),
        out_specs=(P(None, "gx", "gy", None), P(None, "gx", "gy", None)),
        check_vma=False,
    )
```

```python
import functools

import jax
import jax.numpy as jnp
from jax import lax
from jax.experimental import pallas as pl
from jax.experimental.pallas import tpu as pltpu
from jax.sharding import PartitionSpec as P

STEPS = 5
SURF = 5
TIME_STEP = 0.7
EX = 8
EY = 16
NZ = 128
PIECE = 384
MESH = pl.DeviceIdType.MESH
F32 = jnp.float32
BF16 = jnp.bfloat16


def lane_next(v):
    lane = lax.broadcasted_iota(jnp.int32, v.shape, 1)
    return jnp.where(lane < NZ - 1, pltpu.roll(v, NZ - 1, 1), 0.0)


def lane_before(v):
    lane = lax.broadcasted_iota(jnp.int32, v.shape, 1)
    return jnp.where(lane > 0, pltpu.roll(v, 1, 1), 0.0)


def strains(near, far):
    ss, ds, sd = [], [], []
    for c in range(3):
        s0, s1 = near[c][0] + near[c][1], far[c][0] + far[c][1]
        d0, d1 = near[c][1] - near[c][0], far[c][1] - far[c][0]
        ss.append(s0 + s1)
        ds.append(s1 - s0)
        sd.append(d0 + d1)

    def both(v):
        return v + lane_next(v)

    xx = 0.25 * both(ds[0])
    yy = 0.25 * both(sd[1])
    zz = 0.25 * (lane_next(ss[2]) - ss[2])
    xy = 0.125 * both(sd[0] + ds[1])
    yz = 0.125 * (lane_next(ss[1] + sd[2]) + (sd[2] - ss[1]))
    zx = 0.125 * (lane_next(ss[0] + ds[2]) + (ds[2] - ss[0]))
    trace = xx + yy + zz
    mean = trace * (1.0 / 3.0)
    return trace, [xx - mean, yy - mean, zz - mean, xy, yz, zx]


def stresses(trace, dev, read_plastic, write_plastic, read_prop):
    total = [None] * 6
    for s in range(SURF):
        shear2 = read_prop(1 + s)
        ratio = read_prop(1 + SURF + s)
        diff = [dev[k] - read_plastic(6 * s + k) for k in range(6)]
        w = diff[0] * diff[0] + diff[1] * diff[1] + diff[2] * diff[2]
        w = w + 2.0 * (diff[3] * diff[3] + diff[4] * diff[4] + diff[5] * diff[5])
        factor = ratio * lax.rsqrt(jnp.maximum(w, ratio * ratio))
        for k in range(6):
            kept = factor * diff[k]
            write_plastic(6 * s + k, dev[k] - kept)
            part = shear2 * kept
            total[k] = part if total[k] is None else total[k] + part
    pressure = read_prop(0) * trace
    return [total[k] + pressure if k < 3 else total[k] for k in range(6)]


def properties(mat, moduli, radii):
    def pick(table, column):
        value = jnp.full(mat.shape, table[0, column], F32)
        for m in range(1, 8):
            value = jnp.where(mat == float(m), table[m, column], value)
        return value

    shear2 = [2.0 * pick(moduli, 1 + s) for s in range(SURF)]
    ratio = [pick(radii, s) / shear2[s] for s in range(SURF)]
    return [pick(moduli, 0)] + shear2 + ratio


def kernel(
    nx, ny,
    disp, velo, plas, mass, mate, moduli, radii, hist, coef, nodes,
    out_disp, out_plas,
    U, V, W, YH, T, CS, CR, PL, PYS, PY, PCS, PCR, PR, PRY, SIG,
    FS, FR, H, B, A, ACC, WM, hv, cv, ct, nv, velv, massv, matev,
    lsem, osem, a_send, a_recv, h_send, h_recv, p_send, p_recv,
):
    gx = lax.axis_index("gx")
    gy = lax.axis_index("gy")
    xn, xp = lax.rem(gx + 1, nx), lax.rem(gx + nx - 1, nx)
    yn, yp = lax.rem(gy + 1, ny), lax.rem(gy + ny - 1, ny)

    barrier = pltpu.get_barrier_semaphore()

    def greet(k, carry):
        pl.semaphore_signal(
            barrier, inc=1, device_id=(lax.rem(gx + k, nx), gy), device_id_type=MESH
        )
        return carry

    lax.fori_loop(1, nx, greet, 0)
    for place in ((gx, yn), (gx, yp), (xn, yn), (xn, yp), (xp, yn), (xp, yp)):
        pl.semaphore_signal(barrier, inc=1, device_id=place, device_id_type=MESH)

    loads = [
        pltpu.make_async_copy(src, dst, lsem.at[i])
        for i, (src, dst) in enumerate(
            (
                (hist, hv),
                (coef, cv),
                (plas, PL.at[pl.ds(0, 6 * SURF), pl.ds(1, EX)]),
                (disp, U.at[1, :, pl.ds(1, EX), pl.ds(0, EY)]),
                (mate, matev),
                (nodes, nv),
                (velo, velv),
                (mass, massv),
            )
        )
    ]
    for load in loads:
        load.start()

    loads[0].wait()
    loads[1].wait()

    def split_coef(a, carry):
        for j in range(2):
            ct[j, pl.ds(a, 1), :] = cv[a, j : j + 1, :]
        return carry

    lax.fori_loop(0, nx, split_coef, 0, unroll=4)

    def make_forces(g, carry):
        rows = pl.ds(pl.multiple_of(g * 8, 8), 8)
        cm, ck = ct[0, rows, :], ct[1, rows, :]
        for c in range(3):
            h = [hv[c * 7 + l, rows, :] for l in range(STEPS + 2)]
            for n in range(STEPS):
                force = cm * (h[n + 2] - 2.0 * h[n + 1] + h[n]) + ck * h[n + 1]
                for i in range(8):
                    FS[n, g * 8 + i, :, c * PIECE : (c + 1) * PIECE] = force[i : i + 1, :]
        return carry

    lax.fori_loop(0, nx // 8, make_forces, 0)

    def own_forces(n, carry):
        FR[n, gx] = FS[n, gx]
        return carry

    lax.fori_loop(0, STEPS, own_forces, 0)

    pl.semaphore_wait(barrier, nx - 1 + 6)

    def remote(src, dst, send, recv, place):
        return pltpu.make_async_remote_copy(
            src_ref=src, dst_ref=dst, send_sem=send, recv_sem=recv, device_id=place,
            device_id_type=MESH,
        )

    def send_forces(n):
        def one(k, carry):
            to = lax.rem(gx + k, nx)
            remote(FS.at[n, to], FR.at[n, gx], a_send.at[n], a_recv.at[n], (to, gy)).start()
            return carry

        lax.fori_loop(1, nx, one, 0)

    def forces_done(n):
        some = FR.at[n, pl.ds(0, nx - 1)]
        return (
            pltpu.make_async_copy(some, some, a_send.at[n]),
            pltpu.make_async_copy(some, some, a_recv.at[n]),
        )

    def halo(n):
        own = pl.ds(0, EY)
        pairs = (
            (U.at[n + 1, :, 1, own], U.at[n + 1, :, EX + 1, own], (xp, gy)),
            (U.at[n + 1, :, EX, own], U.at[n + 1, :, 0, own], (xn, gy)),
            (V.at[n, :, pl.ds(8, 8)], T.at[n], (gx, yp)),
            (YH.at[n], W.at[n, :, pl.ds(8, 8)], (gx, yn)),
            (CS.at[n, 0], CR.at[n, 0], (xp, yp)),
            (CS.at[n, 1], CR.at[n, 1], (xp, yn)),
            (CS.at[n, 2], CR.at[n, 2], (xn, yp)),
            (CS.at[n, 3], CR.at[n, 3], (xn, yn)),
        )
        return [
            remote(src, dst, h_send.at[n, i], h_recv.at[n, i], place)
            for i, (src, dst, place) in enumerate(pairs)
        ]

    low_x, high_x, low_y, high_y = gx > 0, gx < nx - 1, gy > 0, gy < ny - 1
    leaves = (
        low_x, high_x, low_y, high_y,
        low_x & low_y, low_x & high_y, high_x & low_y, high_x & high_y,
    )
    reaches = (
        high_x, low_x, high_y, low_y,
        high_x & high_y, high_x & low_y, low_x & high_y, low_x & low_y,
    )

    def where_true(copies, flags, act):
        for copy, flag in zip(copies, flags):

            @pl.when(flag)
            def _(copy=copy):
                act(copy)

    def plastic_halo():
        pairs = (
            (PL.at[:, EX], PL.at[:, 0], (xn, gy)),
            (PYS, PY.at[:, pl.ds(8, 8)], (gx, yn)),
            (PCS, PCR, (xn, yn)),
        )
        return [
            remote(src, dst, p_send.at[i], p_recv.at[i], place)
            for i, (src, dst, place) in enumerate(pairs)
        ]

    send_forces(0)

    loads[3].wait()

    def pack_rows(x, carry):
        for c in range(3):
            V[0, c, pl.ds(8 + x, 1), :] = U[1, c, x + 1, 0:1, :]
            YH[0, c, pl.ds(x, 1), :] = U[1, c, x + 1, EY - 1 : EY, :]
        return carry

    lax.fori_loop(0, EX, pack_rows, 0)

    def pack_corners(n):
        CS[n, 0] = V[n, :, 8:9, :]
        CS[n, 1] = YH[n, :, 0:1, :]
        CS[n, 2] = V[n, :, 15:16, :]
        CS[n, 3] = YH[n, :, 7:8, :]

    pack_corners(0)
    where_true(halo(0), leaves, lambda copy: copy.start())

    loads[4].wait()
    PL[6 * SURF, 1 : EX + 1] = matev[...].astype(F32)
    loads[2].wait()

    def pack_plastic(k, carry):
        for x in range(EX):
            PYS[k, x : x + 1, :] = PL[k, x + 1, EY - 1 : EY, :]
        PCS[k] = PYS[k, EX - 1 : EX, :]
        return carry

    lax.fori_loop(0, 6 * SURF + 1, pack_plastic, 0)
    for copy in plastic_halo():
        copy.start()
    send_forces(1)

    loads[5].wait()

    def one_hot(r, carry):
        v = nv[:, pl.ds(pl.multiple_of(r * PIECE, 128), PIECE)]
        high = (v // 2048) * 8 + (v // 128) % 8
        low = ((v // 1024) % 2) * 128 + v % 128
        rows = lax.broadcasted_iota(jnp.int32, (64, PIECE), 0)
        H[r] = jnp.where(rows == high, 1.0, 0.0).astype(BF16)
        rows = lax.broadcasted_iota(jnp.int32, (256, PIECE), 0)
        at = pl.ds(pl.multiple_of(r * PIECE, 128), PIECE)
        B[:, at] = jnp.where(rows == low, 1.0, 0.0).astype(BF16)
        return carry

    lax.fori_loop(0, nx, one_hot, 0)

    def own_props(x, carry):
        for k, value in enumerate(properties(PL[6 * SURF, x], moduli, radii)):
            PR[k, x] = value
        return carry

    lax.fori_loop(1, EX + 1, own_props, 0)

    for load in loads[6:]:
        load.wait()
    WM[...] = (TIME_STEP * TIME_STEP) / massv[...]
    U[0, :, 1 : EX + 1, 0:EY] = U[1, :, 1 : EX + 1, 0:EY] - TIME_STEP * velv[...]

    def scatter(n):
        def spread(r, carry):
            v = jnp.broadcast_to(FR[n, r], (16, 3 * PIECE))
            head = v.astype(BF16)
            tail = (v - head.astype(F32)).astype(BF16)
            at = pl.ds(pl.multiple_of(r * PIECE, 128), PIECE)
            for g in range(4):
                hot = H[r, g * 16 : (g + 1) * 16, :]
                for i, part in enumerate((head, tail)):
                    for c in range(3):
                        top = (i * 3 + c) * 64 + g * 16
                        A[top : top + 16, at] = hot * part[:, c * PIECE : (c + 1) * PIECE]
            return carry

        lax.fori_loop(0, nx, spread, 0, unroll=nx)
        ACC[...] = lax.dot_general(
            A[...], B[...], (((1,), (1,)), ((), ())), preferred_element_type=F32
        )

    outs = [
        pltpu.make_async_copy(
            U.at[STEPS + 1, :, pl.ds(1, EX), pl.ds(0, EY)], out_disp, osem.at[0]
        ),
        pltpu.make_async_copy(PL.at[pl.ds(0, 6 * SURF), pl.ds(1, EX)], out_plas, osem.at[1]),
    ]

    def step(n, carry):
        for copy in forces_done(n):
            copy.wait()
        scatter(n)

        @pl.when(n == 0)
        def _():
            for copy in plastic_halo():
                copy.wait()
            PY[:, 7:8, :] = PCR[...]
            live_x = jnp.where(gx > 0, 1.0, 0.0).astype(F32)
            live_y = jnp.where(gy > 0, 1.0, 0.0).astype(F32)
            for k, value in enumerate(properties(PL[6 * SURF, 0], moduli, radii)):
                PR[k, 0] = value * live_x if k <= SURF else value
            row = lax.broadcasted_iota(jnp.int32, (16, NZ), 0)
            live = jnp.where(row <= 7, live_x * live_y, live_y)
            for k, value in enumerate(properties(PY[6 * SURF], moduli, radii)):
                PRY[k] = value * live if k <= SURF else value

        copies = halo(n)
        where_true(copies, reaches, lambda copy: copy.wait_recv())

        def unpack(x, inner):
            for c in range(3):
                U[n + 1, c, x + 1, EY : EY + 1, :] = T[n, c, pl.ds(x, 1), :]
            return inner

        lax.fori_loop(0, EX, unpack, 0)
        U[n + 1, :, EX + 1, EY : EY + 1, :] = CR[n, 0]
        W[n, :, 16:17, :] = CR[n, 1]
        U[n + 1, :, 0, EY : EY + 1, :] = CR[n, 2]
        W[n, :, 7:8, :] = CR[n, 3]

        @pl.when(gx == 0)
        def _():
            U[n + 1, :, 0] = jnp.zeros((3, EY + 8, NZ), F32)
            W[n, :, 0:8, :] = jnp.zeros((3, 8, NZ), F32)

        @pl.when(gy == 0)
        def _():
            W[n] = jnp.zeros((3, 24, NZ), F32)

        @pl.when(gx == nx - 1)
        def _():
            U[n + 1, :, EX + 1] = jnp.zeros((3, 24, NZ), F32)
            W[n, :, 16:17, :] = jnp.zeros((3, 1, NZ), F32)

        @pl.when(gy == ny - 1)
        def _():
            U[n + 1, :, :, EY : EY + 8] = jnp.zeros((3, EX + 2, 8, NZ), F32)

        V[n, :, 7:8, :] = U[n + 1, :, 0, 0:1, :]
        V[n, :, 16:17, :] = U[n + 1, :, EX + 1, 0:1, :]

        for t in range(2):
            lo = pl.ds(t * 8, 8)
            up = pl.ds(t * 8 + 1, 8)
            near = [(W[n, c, lo, :], V[n, c, lo, :]) for c in range(3)]
            far = [(W[n, c, up, :], V[n, c, up, :]) for c in range(3)]
            trace, dev = strains(near, far)

            def write(k, value):
                PY[k, lo, :] = value

            sigma = stresses(trace, dev, lambda k: PY[k, lo, :], write, lambda k: PRY[k, lo, :])
            for k in range(6):
                if t == 0:
                    SIG[k, 0, 7:8, :] = sigma[k][7:8, :]
                else:
                    for x in range(EX):
                        SIG[k, x + 1, 7:8, :] = sigma[k][x : x + 1, :]

        def elements(x, inner):
            for t in range(2):
                lo = pl.ds(t * 8, 8)
                up = pl.ds(t * 8 + 1, 8)
                near = [(U[n + 1, c, x, lo, :], U[n + 1, c, x, up, :]) for c in range(3)]
                far = [(U[n + 1, c, x + 1, lo, :], U[n + 1, c, x + 1, up, :]) for c in range(3)]
                trace, dev = strains(near, far)

                def write(k, value):
                    PL[k, x, lo, :] = value

                sigma = stresses(
                    trace, dev, lambda k: PL[k, x, lo, :], write, lambda k: PR[k, x, lo, :]
                )
                for k in range(6):
                    SIG[k, x, t * 8 + 8 : t * 8 + 16, :] = sigma[k]
            return inner

        lax.fori_loop(0, EX + 1, elements, 0, unroll=EX + 1)

        @pl.when(n == STEPS - 1)
        def _():
            outs[1].start()

        def update(x, inner):
            for t in range(2):
                old = pl.ds(t * 8 + 7, 8)
                new = pl.ds(t * 8 + 8, 8)
                lo = pl.ds(t * 8, 8)
                minus, plus = {}, {}
                for k in range(6):
                    for rows in (0, 1):
                        at = new if rows else old
                        before, here = SIG[k, x, at, :], SIG[k, x + 1, at, :]
                        plus[k, rows] = before + here
                        if k in (0, 3, 5):
                            minus[k, rows] = before - here
                for c, (kx, ky, kz) in enumerate(((0, 3, 5), (3, 1, 4), (5, 4, 2))):
                    across = (minus[kx, 0] + plus[ky, 0]) + (minus[kx, 1] - plus[ky, 1])
                    down = plus[kz, 0] + plus[kz, 1]
                    inside = lane_before(across + down) + (across - down)
                    top = c * 64 + x * 8
                    lanes = slice(t * 128, (t + 1) * 128)
                    placed = ACC[pl.ds(top, 8), lanes] + ACC[pl.ds(192 + top, 8), lanes]
                    now = U[n + 1, c, x + 1, lo, :]
                    later = (
                        2.0 * now
                        - U[n, c, x + 1, lo, :]
                        + WM[x, lo, :] * (placed - 0.25 * inside)
                    )
                    U[n + 2, c, x + 1, lo, :] = later
                    if t == 0:
                        V[n + 1, c, pl.ds(8 + x, 1), :] = later[0:1, :]
                    else:
                        YH[n + 1, c, pl.ds(x, 1), :] = later[7:8, :]
            return inner

        lax.fori_loop(0, EX, update, 0, unroll=EX)

        @pl.when(n < STEPS - 1)
        def _():
            pack_corners(n + 1)
            where_true(halo(n + 1), leaves, lambda copy: copy.start())

        @pl.when(n < STEPS - 2)
        def _():
            send_forces(n + 2)

        where_true(copies, leaves, lambda copy: copy.wait_send())
        return carry

    lax.fori_loop(0, STEPS, step, 0)
    outs[0].start()
    for out in outs:
        out.wait()


def per_device(nx, ny, *args):
    any_space = pl.BlockSpec(memory_space=pl.ANY)
    smem = pl.BlockSpec(memory_space=pltpu.SMEM)
    vmem = pltpu.VMEM
    dma = pltpu.SemaphoreType.DMA
    scratch = [
        vmem((STEPS + 2, 3, EX + 2, EY + 8, NZ), F32),
        vmem((STEPS + 1, 3, 24, NZ), F32),
        vmem((STEPS, 3, 24, NZ), F32),
        vmem((STEPS + 1, 3, 8, NZ), F32),
        vmem((STEPS, 3, 8, NZ), F32),
        vmem((STEPS, 4, 3, 1, NZ), F32),
        vmem((STEPS, 4, 3, 1, NZ), F32),
        vmem((6 * SURF + 1, EX + 1, EY, NZ), F32),
        vmem((6 * SURF + 1, EX, NZ), F32),
        vmem((6 * SURF + 1, 16, NZ), F32),
        vmem((6 * SURF + 1, 1, NZ), F32),
        vmem((6 * SURF + 1, 1, NZ), F32),
        vmem((1 + 2 * SURF, EX + 1, EY, NZ), F32),
        vmem((1 + 2 * SURF, 16, NZ), F32),
        vmem((6, EX + 1, EY + 8, NZ), F32),
        vmem((STEPS, nx, 1, 3 * PIECE), F32),
        vmem((STEPS, nx, 1, 3 * PIECE), F32),
        vmem((nx, 64, PIECE), BF16),
        vmem((256, nx * PIECE), BF16),
        vmem((384, nx * PIECE), BF16),
        vmem((384, 256), F32),
        vmem((EX, EY, NZ), F32),
        vmem((21, nx, PIECE), F32),
        vmem((nx, 2, PIECE), F32),
        vmem((2, nx, PIECE), F32),
        vmem((1, nx * PIECE), jnp.int32),
        vmem((3, EX, EY, NZ), F32),
        vmem((EX, EY, NZ), F32),
        vmem((EX, EY, NZ), jnp.int32),
        dma((8,)),
        dma((2,)),
        dma((STEPS,)),
        dma((STEPS,)),
        dma((STEPS, 8)),
        dma((STEPS, 8)),
        dma((3,)),
        dma((3,)),
    ]
    return pl.pallas_call(
        functools.partial(kernel, nx, ny),
        out_shape=(
            pltpu.VMEM((3, EX, EY, NZ), F32),
            pltpu.VMEM((6 * SURF, EX, EY, NZ), F32),
        ),
        in_specs=[any_space] * 5 + [smem] * 2 + [any_space] * 3,
        out_specs=(any_space, any_space),
        scratch_shapes=scratch,
        compiler_params=pltpu.CompilerParams(
            collective_id=0, has_side_effects=True, vmem_limit_bytes=60 * 1024 * 1024
        ),
        name="box_steps",
    )(*args[:7], jnp.transpose(args[7], (1, 0, 2)), *args[8:])


def solution(mesh):
    return jax.shard_map(
        functools.partial(per_device, mesh.shape["gx"], mesh.shape["gy"]),
        mesh=mesh,
        in_specs=(
            P(None, "gx", "gy", None),
            P(None, "gx", "gy", None),
            P(None, "gx", "gy", None),
            P("gx", "gy", None),
            P("gx", "gy", None),
            P(),
            P(),
            P("gx", None, "gy"),
            P("gx", None, "gy"),
            P("gx", "gy"),
        ),
        out_specs=(P(None, "gx", "gy", None), P(None, "gx", "gy", None)),
        check_vma=False,
    )
```

```python
import functools

import jax
import jax.numpy as jnp
from jax import lax
from jax.experimental import pallas as pl
from jax.experimental.pallas import tpu as pltpu
from jax.sharding import PartitionSpec as P

STEPS = 5
SURF = 5
TIME_STEP = 0.7
EX = 8
EY = 16
NZ = 128
PIECE = 384
MESH = pl.DeviceIdType.MESH
F32 = jnp.float32
BF16 = jnp.bfloat16


def lane_next(v):
    lane = lax.broadcasted_iota(jnp.int32, v.shape, 1)
    return jnp.where(lane < NZ - 1, pltpu.roll(v, NZ - 1, 1), 0.0)


def lane_before(v):
    lane = lax.broadcasted_iota(jnp.int32, v.shape, 1)
    return jnp.where(lane > 0, pltpu.roll(v, 1, 1), 0.0)


def strains(near, far):
    ss, ds, sd = [], [], []
    for c in range(3):
        s0, s1 = near[c][0] + near[c][1], far[c][0] + far[c][1]
        d0, d1 = near[c][1] - near[c][0], far[c][1] - far[c][0]
        ss.append(s0 + s1)
        ds.append(s1 - s0)
        sd.append(d0 + d1)

    def both(v):
        return v + lane_next(v)

    xx = 0.25 * both(ds[0])
    yy = 0.25 * both(sd[1])
    zz = 0.25 * (lane_next(ss[2]) - ss[2])
    xy = 0.125 * both(sd[0] + ds[1])
    yz = 0.125 * (lane_next(ss[1] + sd[2]) + (sd[2] - ss[1]))
    zx = 0.125 * (lane_next(ss[0] + ds[2]) + (ds[2] - ss[0]))
    trace = xx + yy + zz
    mean = trace * (1.0 / 3.0)
    return trace, [xx - mean, yy - mean, zz - mean, xy, yz, zx]


def stresses(trace, dev, read_plastic, write_plastic, read_prop):
    total = [None] * 6
    for s in range(SURF):
        shear2 = read_prop(1 + s)
        ratio = read_prop(1 + SURF + s)
        diff = [dev[k] - read_plastic(6 * s + k) for k in range(6)]
        w = diff[0] * diff[0] + diff[1] * diff[1] + diff[2] * diff[2]
        w = w + 2.0 * (diff[3] * diff[3] + diff[4] * diff[4] + diff[5] * diff[5])
        factor = ratio * lax.rsqrt(jnp.maximum(w, ratio * ratio))
        for k in range(6):
            kept = factor * diff[k]
            write_plastic(6 * s + k, dev[k] - kept)
            part = shear2 * kept
            total[k] = part if total[k] is None else total[k] + part
    pressure = read_prop(0) * trace
    return [total[k] + pressure if k < 3 else total[k] for k in range(6)]


def properties(mat, moduli, radii):
    def pick(table, column):
        value = jnp.full(mat.shape, table[0, column], F32)
        for m in range(1, 8):
            value = jnp.where(mat == float(m), table[m, column], value)
        return value

    shear2 = [2.0 * pick(moduli, 1 + s) for s in range(SURF)]
    ratio = [pick(radii, s) / shear2[s] for s in range(SURF)]
    return [pick(moduli, 0)] + shear2 + ratio


def kernel(
    nx, ny,
    disp, velo, plas, mass, mate, moduli, radii, hist, coef, nodes,
    out_disp, out_plas,
    U, V, W, YH, T, CS, CR, PL, PYS, PY, PCS, PCR, PR, PRY, SIG,
    FS, FR, H, B, A, ACC, WM, hv, cv, ct, nv, velv, massv, matev,
    lsem, osem, a_send, a_recv, h_send, h_recv, p_send, p_recv,
):
    gx = lax.axis_index("gx")
    gy = lax.axis_index("gy")
    xn, xp = lax.rem(gx + 1, nx), lax.rem(gx + nx - 1, nx)
    yn, yp = lax.rem(gy + 1, ny), lax.rem(gy + ny - 1, ny)

    barrier = pltpu.get_barrier_semaphore()

    def greet(k, carry):
        pl.semaphore_signal(
            barrier, inc=1, device_id=(lax.rem(gx + k, nx), gy), device_id_type=MESH
        )
        return carry

    lax.fori_loop(1, nx, greet, 0)
    for place in ((gx, yn), (gx, yp), (xn, yn), (xn, yp), (xp, yn), (xp, yp)):
        pl.semaphore_signal(barrier, inc=1, device_id=place, device_id_type=MESH)

    loads = [
        pltpu.make_async_copy(src, dst, lsem.at[i])
        for i, (src, dst) in enumerate(
            (
                (hist, hv),
                (coef, cv),
                (plas, PL.at[pl.ds(0, 6 * SURF), pl.ds(1, EX)]),
                (disp, U.at[1, :, pl.ds(1, EX), pl.ds(0, EY)]),
                (mate, matev),
                (nodes, nv),
                (velo, velv),
                (mass, massv),
            )
        )
    ]
    for load in loads:
        load.start()

    loads[0].wait()
    loads[1].wait()

    def split_coef(a, carry):
        for j in range(2):
            ct[j, pl.ds(a, 1), :] = cv[a, j : j + 1, :]
        return carry

    lax.fori_loop(0, nx, split_coef, 0, unroll=4)

    def make_forces(g, carry):
        rows = pl.ds(pl.multiple_of(g * 8, 8), 8)
        cm, ck = ct[0, rows, :], ct[1, rows, :]
        for c in range(3):
            h = [hv[c * 7 + l, rows, :] for l in range(STEPS + 2)]
            for n in range(STEPS):
                force = cm * (h[n + 2] - 2.0 * h[n + 1] + h[n]) + ck * h[n + 1]
                for i in range(8):
                    FS[n, g * 8 + i, :, c * PIECE : (c + 1) * PIECE] = force[i : i + 1, :]
        return carry

    lax.fori_loop(0, nx // 8, make_forces, 0)

    def own_forces(n, carry):
        FR[n, gx] = FS[n, gx]
        return carry

    lax.fori_loop(0, STEPS, own_forces, 0)

    pl.semaphore_wait(barrier, nx - 1 + 6)

    def remote(src, dst, send, recv, place):
        return pltpu.make_async_remote_copy(
            src_ref=src, dst_ref=dst, send_sem=send, recv_sem=recv, device_id=place,
            device_id_type=MESH,
        )

    def send_forces(n):
        def one(k, carry):
            to = jnp.where(gx + k < nx, gx + k, gx + k - nx)
            remote(FS.at[n, to], FR.at[n, gx], a_send.at[n], a_recv.at[n], (to, gy)).start()
            return carry

        lax.fori_loop(1, nx, one, 0, unroll=nx - 1)

    def forces_done(n):
        some = FR.at[n, pl.ds(0, nx - 1)]
        return (
            pltpu.make_async_copy(some, some, a_send.at[n]),
            pltpu.make_async_copy(some, some, a_recv.at[n]),
        )

    def halo(n):
        own = pl.ds(0, EY)
        pairs = (
            (U.at[n + 1, :, 1, own], U.at[n + 1, :, EX + 1, own], (xp, gy)),
            (U.at[n + 1, :, EX, own], U.at[n + 1, :, 0, own], (xn, gy)),
            (V.at[n, :, pl.ds(8, 8)], T.at[n], (gx, yp)),
            (YH.at[n], W.at[n, :, pl.ds(8, 8)], (gx, yn)),
            (CS.at[n, 0], CR.at[n, 0], (xp, yp)),
            (CS.at[n, 1], CR.at[n, 1], (xp, yn)),
            (CS.at[n, 2], CR.at[n, 2], (xn, yp)),
            (CS.at[n, 3], CR.at[n, 3], (xn, yn)),
        )
        return [
            remote(src, dst, h_send.at[n, i], h_recv.at[n, i], place)
            for i, (src, dst, place) in enumerate(pairs)
        ]

    low_x, high_x, low_y, high_y = gx > 0, gx < nx - 1, gy > 0, gy < ny - 1
    leaves = (
        low_x, high_x, low_y, high_y,
        low_x & low_y, low_x & high_y, high_x & low_y, high_x & high_y,
    )
    reaches = (
        high_x, low_x, high_y, low_y,
        high_x & high_y, high_x & low_y, low_x & high_y, low_x & low_y,
    )

    def where_true(copies, flags, act):
        for copy, flag in zip(copies, flags):

            @pl.when(flag)
            def _(copy=copy):
                act(copy)

    def plastic_halo():
        pairs = (
            (PL.at[:, EX], PL.at[:, 0], (xn, gy)),
            (PYS, PY.at[:, pl.ds(8, 8)], (gx, yn)),
            (PCS, PCR, (xn, yn)),
        )
        return [
            remote(src, dst, p_send.at[i], p_recv.at[i], place)
            for i, (src, dst, place) in enumerate(pairs)
        ]

    send_forces(0)

    loads[3].wait()

    def pack_rows(x, carry):
        for c in range(3):
            V[0, c, pl.ds(8 + x, 1), :] = U[1, c, x + 1, 0:1, :]
            YH[0, c, pl.ds(x, 1), :] = U[1, c, x + 1, EY - 1 : EY, :]
        return carry

    lax.fori_loop(0, EX, pack_rows, 0)

    def pack_corners(n):
        CS[n, 0] = V[n, :, 8:9, :]
        CS[n, 1] = YH[n, :, 0:1, :]
        CS[n, 2] = V[n, :, 15:16, :]
        CS[n, 3] = YH[n, :, 7:8, :]

    pack_corners(0)
    where_true(halo(0), leaves, lambda copy: copy.start())

    loads[4].wait()
    PL[6 * SURF, 1 : EX + 1] = matev[...].astype(F32)
    loads[2].wait()

    def pack_plastic(k, carry):
        for x in range(EX):
            PYS[k, x : x + 1, :] = PL[k, x + 1, EY - 1 : EY, :]
        PCS[k] = PYS[k, EX - 1 : EX, :]
        return carry

    lax.fori_loop(0, 6 * SURF + 1, pack_plastic, 0)
    for copy in plastic_halo():
        copy.start()
    send_forces(1)
    send_forces(2)

    loads[5].wait()

    def one_hot(r, carry):
        v = nv[:, pl.ds(pl.multiple_of(r * PIECE, 128), PIECE)]
        high = (v // 2048) * 8 + (v // 128) % 8
        low = ((v // 1024) % 2) * 128 + v % 128
        rows = lax.broadcasted_iota(jnp.int32, (64, PIECE), 0)
        H[r] = jnp.where(rows == high, 1.0, 0.0).astype(BF16)
        rows = lax.broadcasted_iota(jnp.int32, (256, PIECE), 0)
        at = pl.ds(pl.multiple_of(r * PIECE, 128), PIECE)
        B[:, at] = jnp.where(rows == low, 1.0, 0.0).astype(BF16)
        return carry

    lax.fori_loop(0, nx, one_hot, 0)

    def own_props(x, carry):
        for k, value in enumerate(properties(PL[6 * SURF, x], moduli, radii)):
            PR[k, x] = value
        return carry

    lax.fori_loop(1, EX + 1, own_props, 0)

    for load in loads[6:]:
        load.wait()
    WM[...] = (TIME_STEP * TIME_STEP) / massv[...]
    U[0, :, 1 : EX + 1, 0:EY] = U[1, :, 1 : EX + 1, 0:EY] - TIME_STEP * velv[...]

    def scatter(n):
        def spread(r, carry):
            v = jnp.broadcast_to(FR[n, r], (16, 3 * PIECE))
            head = v.astype(BF16)
            tail = (v - head.astype(F32)).astype(BF16)
            at = pl.ds(pl.multiple_of(r * PIECE, 128), PIECE)
            for g in range(4):
                hot = H[r, g * 16 : (g + 1) * 16, :]
                for i, part in enumerate((head, tail)):
                    for c in range(3):
                        top = (i * 3 + c) * 64 + g * 16
                        A[top : top + 16, at] = hot * part[:, c * PIECE : (c + 1) * PIECE]
            return carry

        lax.fori_loop(0, nx, spread, 0, unroll=nx)
        ACC[...] = lax.dot_general(
            A[...], B[...], (((1,), (1,)), ((), ())), preferred_element_type=F32
        )

    outs = [
        pltpu.make_async_copy(
            U.at[STEPS + 1, :, pl.ds(1, EX), pl.ds(0, EY)], out_disp, osem.at[0]
        ),
        pltpu.make_async_copy(PL.at[pl.ds(0, 6 * SURF), pl.ds(1, EX)], out_plas, osem.at[1]),
    ]

    def element(n, x, t):
        lo = pl.ds(t * 8, 8)
        up = pl.ds(t * 8 + 1, 8)
        near = [(U[n + 1, c, x, lo, :], U[n + 1, c, x, up, :]) for c in range(3)]
        far = [(U[n + 1, c, x + 1, lo, :], U[n + 1, c, x + 1, up, :]) for c in range(3)]
        trace, dev = strains(near, far)

        def write(k, value):
            PL[k, x, lo, :] = value

        sigma = stresses(
            trace, dev, lambda k: PL[k, x, lo, :], write, lambda k: PR[k, x, lo, :]
        )
        for k in range(6):
            SIG[k, x, t * 8 + 8 : t * 8 + 16, :] = sigma[k]

    def step(n, carry):
        for copy in forces_done(n):
            copy.wait()
        def inside(x, inner):
            element(n, x, 0)
            return inner

        lax.fori_loop(1, EX, inside, 0, unroll=EX - 1)
        scatter(n)

        @pl.when(n == 0)
        def _():
            for copy in plastic_halo():
                copy.wait()
            PY[:, 7:8, :] = PCR[...]
            live_x = jnp.where(gx > 0, 1.0, 0.0).astype(F32)
            live_y = jnp.where(gy > 0, 1.0, 0.0).astype(F32)
            for k, value in enumerate(properties(PL[6 * SURF, 0], moduli, radii)):
                PR[k, 0] = value * live_x if k <= SURF else value
            row = lax.broadcasted_iota(jnp.int32, (16, NZ), 0)
            live = jnp.where(row <= 7, live_x * live_y, live_y)
            for k, value in enumerate(properties(PY[6 * SURF], moduli, radii)):
                PRY[k] = value * live if k <= SURF else value

        copies = halo(n)
        where_true(copies, reaches, lambda copy: copy.wait_recv())

        def unpack(x, inner):
            for c in range(3):
                U[n + 1, c, x + 1, EY : EY + 1, :] = T[n, c, pl.ds(x, 1), :]
            return inner

        lax.fori_loop(0, EX, unpack, 0)
        U[n + 1, :, EX + 1, EY : EY + 1, :] = CR[n, 0]
        W[n, :, 16:17, :] = CR[n, 1]
        U[n + 1, :, 0, EY : EY + 1, :] = CR[n, 2]
        W[n, :, 7:8, :] = CR[n, 3]

        @pl.when(gx == 0)
        def _():
            U[n + 1, :, 0] = jnp.zeros((3, EY + 8, NZ), F32)
            W[n, :, 0:8, :] = jnp.zeros((3, 8, NZ), F32)

        @pl.when(gy == 0)
        def _():
            W[n] = jnp.zeros((3, 24, NZ), F32)

        @pl.when(gx == nx - 1)
        def _():
            U[n + 1, :, EX + 1] = jnp.zeros((3, 24, NZ), F32)
            W[n, :, 16:17, :] = jnp.zeros((3, 1, NZ), F32)

        @pl.when(gy == ny - 1)
        def _():
            U[n + 1, :, :, EY : EY + 8] = jnp.zeros((3, EX + 2, 8, NZ), F32)

        V[n, :, 7:8, :] = U[n + 1, :, 0, 0:1, :]
        V[n, :, 16:17, :] = U[n + 1, :, EX + 1, 0:1, :]

        for t in range(2):
            lo = pl.ds(t * 8, 8)
            up = pl.ds(t * 8 + 1, 8)
            near = [(W[n, c, lo, :], V[n, c, lo, :]) for c in range(3)]
            far = [(W[n, c, up, :], V[n, c, up, :]) for c in range(3)]
            trace, dev = strains(near, far)

            def write(k, value):
                PY[k, lo, :] = value

            sigma = stresses(trace, dev, lambda k: PY[k, lo, :], write, lambda k: PRY[k, lo, :])
            for k in range(6):
                if t == 0:
                    SIG[k, 0, 7:8, :] = sigma[k][7:8, :]
                else:
                    for x in range(EX):
                        SIG[k, x + 1, 7:8, :] = sigma[k][x : x + 1, :]

        def outside(x, inner):
            element(n, x, 1)
            return inner

        element(n, 0, 0)
        element(n, EX, 0)
        lax.fori_loop(0, EX + 1, outside, 0, unroll=EX + 1)

        @pl.when(n == STEPS - 1)
        def _():
            outs[1].start()

        def update(x, inner):
            for t in range(2):
                old = pl.ds(t * 8 + 7, 8)
                new = pl.ds(t * 8 + 8, 8)
                lo = pl.ds(t * 8, 8)
                minus, plus = {}, {}
                for k in range(6):
                    for rows in (0, 1):
                        at = new if rows else old
                        before, here = SIG[k, x, at, :], SIG[k, x + 1, at, :]
                        plus[k, rows] = before + here
                        if k in (0, 3, 5):
                            minus[k, rows] = before - here
                for c, (kx, ky, kz) in enumerate(((0, 3, 5), (3, 1, 4), (5, 4, 2))):
                    across = (minus[kx, 0] + plus[ky, 0]) + (minus[kx, 1] - plus[ky, 1])
                    down = plus[kz, 0] + plus[kz, 1]
                    inside = lane_before(across + down) + (across - down)
                    top = c * 64 + x * 8
                    lanes = slice(t * 128, (t + 1) * 128)
                    placed = ACC[pl.ds(top, 8), lanes] + ACC[pl.ds(192 + top, 8), lanes]
                    now = U[n + 1, c, x + 1, lo, :]
                    later = (
                        2.0 * now
                        - U[n, c, x + 1, lo, :]
                        + WM[x, lo, :] * (placed - 0.25 * inside)
                    )
                    U[n + 2, c, x + 1, lo, :] = later
                    if t == 0:
                        V[n + 1, c, pl.ds(8 + x, 1), :] = later[0:1, :]
                    else:
                        YH[n + 1, c, pl.ds(x, 1), :] = later[7:8, :]
            return inner

        lax.fori_loop(0, EX, update, 0, unroll=EX)

        @pl.when(n < STEPS - 1)
        def _():
            pack_corners(n + 1)
            where_true(halo(n + 1), leaves, lambda copy: copy.start())

        @pl.when(n < STEPS - 3)
        def _():
            send_forces(n + 3)

        where_true(copies, leaves, lambda copy: copy.wait_send())
        return carry

    lax.fori_loop(0, STEPS, step, 0)
    outs[0].start()
    for out in outs:
        out.wait()


def per_device(nx, ny, *args):
    any_space = pl.BlockSpec(memory_space=pl.ANY)
    smem = pl.BlockSpec(memory_space=pltpu.SMEM)
    vmem = pltpu.VMEM
    dma = pltpu.SemaphoreType.DMA
    scratch = [
        vmem((STEPS + 2, 3, EX + 2, EY + 8, NZ), F32),
        vmem((STEPS + 1, 3, 24, NZ), F32),
        vmem((STEPS, 3, 24, NZ), F32),
        vmem((STEPS + 1, 3, 8, NZ), F32),
        vmem((STEPS, 3, 8, NZ), F32),
        vmem((STEPS, 4, 3, 1, NZ), F32),
        vmem((STEPS, 4, 3, 1, NZ), F32),
        vmem((6 * SURF + 1, EX + 1, EY, NZ), F32),
        vmem((6 * SURF + 1, EX, NZ), F32),
        vmem((6 * SURF + 1, 16, NZ), F32),
        vmem((6 * SURF + 1, 1, NZ), F32),
        vmem((6 * SURF + 1, 1, NZ), F32),
        vmem((1 + 2 * SURF, EX + 1, EY, NZ), F32),
        vmem((1 + 2 * SURF, 16, NZ), F32),
        vmem((6, EX + 1, EY + 8, NZ), F32),
        vmem((STEPS, nx, 1, 3 * PIECE), F32),
        vmem((STEPS, nx, 1, 3 * PIECE), F32),
        vmem((nx, 64, PIECE), BF16),
        vmem((256, nx * PIECE), BF16),
        vmem((384, nx * PIECE), BF16),
        vmem((384, 256), F32),
        vmem((EX, EY, NZ), F32),
        vmem((21, nx, PIECE), F32),
        vmem((nx, 2, PIECE), F32),
        vmem((2, nx, PIECE), F32),
        vmem((1, nx * PIECE), jnp.int32),
        vmem((3, EX, EY, NZ), F32),
        vmem((EX, EY, NZ), F32),
        vmem((EX, EY, NZ), jnp.int32),
        dma((8,)),
        dma((2,)),
        dma((STEPS,)),
        dma((STEPS,)),
        dma((STEPS, 8)),
        dma((STEPS, 8)),
        dma((3,)),
        dma((3,)),
    ]
    return pl.pallas_call(
        functools.partial(kernel, nx, ny),
        out_shape=(
            pltpu.VMEM((3, EX, EY, NZ), F32),
            pltpu.VMEM((6 * SURF, EX, EY, NZ), F32),
        ),
        in_specs=[any_space] * 5 + [smem] * 2 + [any_space] * 3,
        out_specs=(any_space, any_space),
        scratch_shapes=scratch,
        compiler_params=pltpu.CompilerParams(
            collective_id=0, has_side_effects=True, vmem_limit_bytes=60 * 1024 * 1024
        ),
        name="box_steps",
    )(*args[:7], jnp.transpose(args[7], (1, 0, 2)), *args[8:])


def solution(mesh):
    return jax.shard_map(
        functools.partial(per_device, mesh.shape["gx"], mesh.shape["gy"]),
        mesh=mesh,
        in_specs=(
            P(None, "gx", "gy", None),
            P(None, "gx", "gy", None),
            P(None, "gx", "gy", None),
            P("gx", "gy", None),
            P("gx", "gy", None),
            P(),
            P(),
            P("gx", None, "gy"),
            P("gx", None, "gy"),
            P("gx", "gy"),
        ),
        out_specs=(P(None, "gx", "gy", None), P(None, "gx", "gy", None)),
        check_vma=False,
    )
```

```python
import functools

import jax
import jax.numpy as jnp
from jax import lax
from jax.experimental import pallas as pl
from jax.experimental.pallas import tpu as pltpu
from jax.sharding import PartitionSpec as P

STEPS = 5
SURF = 5
TIME_STEP = 0.7
EX = 8
EY = 16
NZ = 128
PIECE = 384
MESH = pl.DeviceIdType.MESH
F32 = jnp.float32
BF16 = jnp.bfloat16


def lane_next(v):
    lane = lax.broadcasted_iota(jnp.int32, v.shape, 1)
    return jnp.where(lane < NZ - 1, pltpu.roll(v, NZ - 1, 1), 0.0)


def lane_before(v):
    lane = lax.broadcasted_iota(jnp.int32, v.shape, 1)
    return jnp.where(lane > 0, pltpu.roll(v, 1, 1), 0.0)


def strains(near, far):
    ss, ds, sd = [], [], []
    for c in range(3):
        s0, s1 = near[c][0] + near[c][1], far[c][0] + far[c][1]
        d0, d1 = near[c][1] - near[c][0], far[c][1] - far[c][0]
        ss.append(s0 + s1)
        ds.append(s1 - s0)
        sd.append(d0 + d1)

    def both(v):
        return v + lane_next(v)

    xx = 0.25 * both(ds[0])
    yy = 0.25 * both(sd[1])
    zz = 0.25 * (lane_next(ss[2]) - ss[2])
    xy = 0.125 * both(sd[0] + ds[1])
    yz = 0.125 * (lane_next(ss[1] + sd[2]) + (sd[2] - ss[1]))
    zx = 0.125 * (lane_next(ss[0] + ds[2]) + (ds[2] - ss[0]))
    trace = xx + yy + zz
    mean = trace * (1.0 / 3.0)
    return trace, [xx - mean, yy - mean, zz - mean, xy, yz, zx]


def stresses(trace, dev, read_plastic, write_plastic, read_prop):
    total = [None] * 6
    for s in range(SURF):
        shear2 = read_prop(1 + s)
        ratio = read_prop(1 + SURF + s)
        diff = [dev[k] - read_plastic(6 * s + k) for k in range(6)]
        w = diff[0] * diff[0] + diff[1] * diff[1] + diff[2] * diff[2]
        w = w + 2.0 * (diff[3] * diff[3] + diff[4] * diff[4] + diff[5] * diff[5])
        factor = ratio * lax.rsqrt(jnp.maximum(w, ratio * ratio))
        for k in range(6):
            kept = factor * diff[k]
            write_plastic(6 * s + k, dev[k] - kept)
            part = shear2 * kept
            total[k] = part if total[k] is None else total[k] + part
    pressure = read_prop(0) * trace
    return [total[k] + pressure if k < 3 else total[k] for k in range(6)]


def properties(mat, moduli, radii):
    def pick(table, column):
        value = jnp.full(mat.shape, table[0, column], F32)
        for m in range(1, 8):
            value = jnp.where(mat == float(m), table[m, column], value)
        return value

    shear2 = [2.0 * pick(moduli, 1 + s) for s in range(SURF)]
    ratio = [pick(radii, s) / shear2[s] for s in range(SURF)]
    return [pick(moduli, 0)] + shear2 + ratio


def kernel(
    nx, ny,
    disp, velo, plas, mass, mate, moduli, radii, hist, coef, nodes,
    out_disp, out_plas,
    U, V, W, YH, T, CS, CR, PL, PYS, PY, PCS, PCR, PR, PRY, SIG,
    FS, FR, H, B, A, ACC, WM, hv, cv, ct, nv, velv, massv, matev,
    lsem, osem, a_send, a_recv, h_send, h_recv, p_send, p_recv,
):
    gx = lax.axis_index("gx")
    gy = lax.axis_index("gy")
    xn, xp = lax.rem(gx + 1, nx), lax.rem(gx + nx - 1, nx)
    yn, yp = lax.rem(gy + 1, ny), lax.rem(gy + ny - 1, ny)

    barrier = pltpu.get_barrier_semaphore()

    def greet(k, carry):
        pl.semaphore_signal(
            barrier, inc=1, device_id=(lax.rem(gx + k, nx), gy), device_id_type=MESH
        )
        return carry

    lax.fori_loop(1, nx, greet, 0)
    for place in ((gx, yn), (gx, yp), (xn, yn), (xn, yp), (xp, yn), (xp, yp)):
        pl.semaphore_signal(barrier, inc=1, device_id=place, device_id_type=MESH)

    loads = [
        pltpu.make_async_copy(src, dst, lsem.at[i])
        for i, (src, dst) in enumerate(
            (
                (hist, hv),
                (coef, cv),
                (plas, PL.at[pl.ds(0, 6 * SURF), pl.ds(1, EX)]),
                (disp, U.at[1, :, pl.ds(1, EX), pl.ds(0, EY)]),
                (mate, matev),
                (nodes, nv),
                (velo, velv),
                (mass, massv),
            )
        )
    ]
    for load in loads:
        load.start()

    loads[0].wait()
    loads[1].wait()

    def split_coef(a, carry):
        for j in range(2):
            ct[j, pl.ds(a, 1), :] = cv[a, j : j + 1, :]
        return carry

    lax.fori_loop(0, nx, split_coef, 0, unroll=4)

    def make_forces(g, carry):
        rows = pl.ds(pl.multiple_of(g * 8, 8), 8)
        cm, ck = ct[0, rows, :], ct[1, rows, :]
        for c in range(3):
            h = [hv[c * 7 + l, rows, :] for l in range(STEPS + 2)]
            for n in range(STEPS):
                force = cm * (h[n + 2] - 2.0 * h[n + 1] + h[n]) + ck * h[n + 1]
                for i in range(8):
                    FS[n, g * 8 + i, :, c * PIECE : (c + 1) * PIECE] = force[i : i + 1, :]
        return carry

    lax.fori_loop(0, nx // 8, make_forces, 0)

    def own_forces(n, carry):
        FR[n, gx] = FS[n, gx]
        return carry

    lax.fori_loop(0, STEPS, own_forces, 0)

    pl.semaphore_wait(barrier, nx - 1 + 6)

    def remote(src, dst, send, recv, place):
        return pltpu.make_async_remote_copy(
            src_ref=src, dst_ref=dst, send_sem=send, recv_sem=recv, device_id=place,
            device_id_type=MESH,
        )

    def send_forces(n):
        def one(k, carry):
            to = jnp.where(gx + k < nx, gx + k, gx + k - nx)
            remote(FS.at[n, to], FR.at[n, gx], a_send.at[n], a_recv.at[n], (to, gy)).start()
            return carry

        lax.fori_loop(1, nx, one, 0, unroll=nx - 1)

    def forces_done(n):
        some = FR.at[n, pl.ds(0, nx - 1)]
        return (
            pltpu.make_async_copy(some, some, a_send.at[n]),
            pltpu.make_async_copy(some, some, a_recv.at[n]),
        )

    def halo(n):
        own = pl.ds(0, EY)
        pairs = (
            (U.at[n + 1, :, 1, own], U.at[n + 1, :, EX + 1, own], (xp, gy)),
            (U.at[n + 1, :, EX, own], U.at[n + 1, :, 0, own], (xn, gy)),
            (V.at[n, :, pl.ds(8, 8)], T.at[n], (gx, yp)),
            (YH.at[n], W.at[n, :, pl.ds(8, 8)], (gx, yn)),
            (CS.at[n, 0], CR.at[n, 0], (xp, yp)),
            (CS.at[n, 1], CR.at[n, 1], (xp, yn)),
            (CS.at[n, 2], CR.at[n, 2], (xn, yp)),
            (CS.at[n, 3], CR.at[n, 3], (xn, yn)),
        )
        return [
            remote(src, dst, h_send.at[n, i], h_recv.at[n, i], place)
            for i, (src, dst, place) in enumerate(pairs)
        ]

    low_x, high_x, low_y, high_y = gx > 0, gx < nx - 1, gy > 0, gy < ny - 1
    leaves = (
        low_x, high_x, low_y, high_y,
        low_x & low_y, low_x & high_y, high_x & low_y, high_x & high_y,
    )
    reaches = (
        high_x, low_x, high_y, low_y,
        high_x & high_y, high_x & low_y, low_x & high_y, low_x & low_y,
    )

    def where_true(copies, flags, act):
        for copy, flag in zip(copies, flags):

            @pl.when(flag)
            def _(copy=copy):
                act(copy)

    def plastic_halo():
        pairs = (
            (PL.at[:, EX], PL.at[:, 0], (xn, gy)),
            (PYS, PY.at[:, pl.ds(8, 8)], (gx, yn)),
            (PCS, PCR, (xn, yn)),
        )
        return [
            remote(src, dst, p_send.at[i], p_recv.at[i], place)
            for i, (src, dst, place) in enumerate(pairs)
        ]

    send_forces(0)

    loads[3].wait()

    def pack_rows(x, carry):
        for c in range(3):
            V[0, c, pl.ds(8 + x, 1), :] = U[1, c, x + 1, 0:1, :]
            YH[0, c, pl.ds(x, 1), :] = U[1, c, x + 1, EY - 1 : EY, :]
        return carry

    lax.fori_loop(0, EX, pack_rows, 0)

    def pack_corners(n):
        CS[n, 0] = V[n, :, 8:9, :]
        CS[n, 1] = YH[n, :, 0:1, :]
        CS[n, 2] = V[n, :, 15:16, :]
        CS[n, 3] = YH[n, :, 7:8, :]

    pack_corners(0)
    where_true(halo(0), leaves, lambda copy: copy.start())

    loads[4].wait()
    PL[6 * SURF, 1 : EX + 1] = matev[...].astype(F32)
    loads[2].wait()

    def pack_plastic(k, carry):
        for x in range(EX):
            PYS[k, x : x + 1, :] = PL[k, x + 1, EY - 1 : EY, :]
        PCS[k] = PYS[k, EX - 1 : EX, :]
        return carry

    lax.fori_loop(0, 6 * SURF + 1, pack_plastic, 0)
    for copy in plastic_halo():
        copy.start()
    send_forces(1)
    send_forces(2)

    loads[5].wait()

    def one_hot(r, carry):
        v = nv[:, pl.ds(pl.multiple_of(r * PIECE, 128), PIECE)]
        high = (v // 2048) * 8 + (v // 128) % 8
        low = ((v // 1024) % 2) * 128 + v % 128
        rows = lax.broadcasted_iota(jnp.int32, (64, PIECE), 0)
        H[r] = jnp.where(rows == high, 1.0, 0.0).astype(BF16)
        rows = lax.broadcasted_iota(jnp.int32, (256, PIECE), 0)
        at = pl.ds(pl.multiple_of(r * PIECE, 128), PIECE)
        B[:, at] = jnp.where(rows == low, 1.0, 0.0).astype(BF16)
        return carry

    lax.fori_loop(0, nx, one_hot, 0)

    def own_props(x, carry):
        for k, value in enumerate(properties(PL[6 * SURF, x], moduli, radii)):
            PR[k, x] = value
        return carry

    lax.fori_loop(1, EX + 1, own_props, 0)

    for load in loads[6:]:
        load.wait()
    WM[...] = (TIME_STEP * TIME_STEP) / massv[...]
    U[0, :, 1 : EX + 1, 0:EY] = U[1, :, 1 : EX + 1, 0:EY] - TIME_STEP * velv[...]

    def scatter(n):
        def spread(r, carry):
            v = jnp.broadcast_to(FR[n, r], (16, 3 * PIECE))
            head = v.astype(BF16)
            tail = (v - head.astype(F32)).astype(BF16)
            at = pl.ds(pl.multiple_of(r * PIECE, 128), PIECE)
            for g in range(4):
                hot = H[r, g * 16 : (g + 1) * 16, :]
                for i, part in enumerate((head, tail)):
                    for c in range(3):
                        top = (i * 3 + c) * 64 + g * 16
                        A[top : top + 16, at] = hot * part[:, c * PIECE : (c + 1) * PIECE]
            return carry

        lax.fori_loop(0, nx, spread, 0, unroll=nx)
        ACC[...] = lax.dot_general(
            A[...], B[...], (((1,), (1,)), ((), ())), preferred_element_type=F32
        )

    outs = [
        pltpu.make_async_copy(
            U.at[STEPS + 1, :, pl.ds(1, EX), pl.ds(0, EY)], out_disp, osem.at[0]
        ),
        pltpu.make_async_copy(
            PL.at[pl.ds(0, 6 * SURF), pl.ds(1, EX - 1), pl.ds(0, 8)],
            out_plas.at[:, pl.ds(0, EX - 1), pl.ds(0, 8)],
            osem.at[1],
        ),
        pltpu.make_async_copy(
            PL.at[pl.ds(0, 6 * SURF), pl.ds(1, EX - 1), pl.ds(8, 8)],
            out_plas.at[:, pl.ds(0, EX - 1), pl.ds(8, 8)],
            osem.at[2],
        ),
        pltpu.make_async_copy(
            PL.at[pl.ds(0, 6 * SURF), EX], out_plas.at[:, EX - 1], osem.at[3]
        ),
    ]

    def element(n, x, t):
        lo = pl.ds(t * 8, 8)
        up = pl.ds(t * 8 + 1, 8)
        near = [(U[n + 1, c, x, lo, :], U[n + 1, c, x, up, :]) for c in range(3)]
        far = [(U[n + 1, c, x + 1, lo, :], U[n + 1, c, x + 1, up, :]) for c in range(3)]
        trace, dev = strains(near, far)

        def write(k, value):
            PL[k, x, lo, :] = value

        sigma = stresses(
            trace, dev, lambda k: PL[k, x, lo, :], write, lambda k: PR[k, x, lo, :]
        )
        for k in range(6):
            SIG[k, x, t * 8 + 8 : t * 8 + 16, :] = sigma[k]

    def step(n, carry):
        for copy in forces_done(n):
            copy.wait()
        def inside(x, inner):
            element(n, x, 0)
            return inner

        lax.fori_loop(1, EX, inside, 0, unroll=EX - 1)
        scatter(n)

        @pl.when(n == STEPS - 1)
        def _():
            outs[1].start()


        @pl.when(n == 0)
        def _():
            for copy in plastic_halo():
                copy.wait()
            PY[:, 7:8, :] = PCR[...]
            live_x = jnp.where(gx > 0, 1.0, 0.0).astype(F32)
            live_y = jnp.where(gy > 0, 1.0, 0.0).astype(F32)
            for k, value in enumerate(properties(PL[6 * SURF, 0], moduli, radii)):
                PR[k, 0] = value * live_x if k <= SURF else value
            row = lax.broadcasted_iota(jnp.int32, (16, NZ), 0)
            live = jnp.where(row <= 7, live_x * live_y, live_y)
            for k, value in enumerate(properties(PY[6 * SURF], moduli, radii)):
                PRY[k] = value * live if k <= SURF else value

        copies = halo(n)
        where_true(copies, reaches, lambda copy: copy.wait_recv())

        def unpack(x, inner):
            for c in range(3):
                U[n + 1, c, x + 1, EY : EY + 1, :] = T[n, c, pl.ds(x, 1), :]
            return inner

        lax.fori_loop(0, EX, unpack, 0)
        U[n + 1, :, EX + 1, EY : EY + 1, :] = CR[n, 0]
        W[n, :, 16:17, :] = CR[n, 1]
        U[n + 1, :, 0, EY : EY + 1, :] = CR[n, 2]
        W[n, :, 7:8, :] = CR[n, 3]

        @pl.when(gx == 0)
        def _():
            U[n + 1, :, 0] = jnp.zeros((3, EY + 8, NZ), F32)
            W[n, :, 0:8, :] = jnp.zeros((3, 8, NZ), F32)

        @pl.when(gy == 0)
        def _():
            W[n] = jnp.zeros((3, 24, NZ), F32)

        @pl.when(gx == nx - 1)
        def _():
            U[n + 1, :, EX + 1] = jnp.zeros((3, 24, NZ), F32)
            W[n, :, 16:17, :] = jnp.zeros((3, 1, NZ), F32)

        @pl.when(gy == ny - 1)
        def _():
            U[n + 1, :, :, EY : EY + 8] = jnp.zeros((3, EX + 2, 8, NZ), F32)

        V[n, :, 7:8, :] = U[n + 1, :, 0, 0:1, :]
        V[n, :, 16:17, :] = U[n + 1, :, EX + 1, 0:1, :]

        for t in range(2):
            lo = pl.ds(t * 8, 8)
            up = pl.ds(t * 8 + 1, 8)
            near = [(W[n, c, lo, :], V[n, c, lo, :]) for c in range(3)]
            far = [(W[n, c, up, :], V[n, c, up, :]) for c in range(3)]
            trace, dev = strains(near, far)

            def write(k, value):
                PY[k, lo, :] = value

            sigma = stresses(trace, dev, lambda k: PY[k, lo, :], write, lambda k: PRY[k, lo, :])
            for k in range(6):
                if t == 0:
                    SIG[k, 0, 7:8, :] = sigma[k][7:8, :]
                else:
                    for x in range(EX):
                        SIG[k, x + 1, 7:8, :] = sigma[k][x : x + 1, :]

        def outside(x, inner):
            element(n, x, 1)
            return inner

        element(n, 0, 0)
        element(n, EX, 0)
        lax.fori_loop(0, EX + 1, outside, 0, unroll=EX + 1)

        @pl.when(n == STEPS - 1)
        def _():
            outs[2].start()
            outs[3].start()

        def update(x, inner):
            for t in range(2):
                old = pl.ds(t * 8 + 7, 8)
                new = pl.ds(t * 8 + 8, 8)
                lo = pl.ds(t * 8, 8)
                minus, plus = {}, {}
                for k in range(6):
                    for rows in (0, 1):
                        at = new if rows else old
                        before, here = SIG[k, x, at, :], SIG[k, x + 1, at, :]
                        plus[k, rows] = before + here
                        if k in (0, 3, 5):
                            minus[k, rows] = before - here
                for c, (kx, ky, kz) in enumerate(((0, 3, 5), (3, 1, 4), (5, 4, 2))):
                    across = (minus[kx, 0] + plus[ky, 0]) + (minus[kx, 1] - plus[ky, 1])
                    down = plus[kz, 0] + plus[kz, 1]
                    inside = lane_before(across + down) + (across - down)
                    top = c * 64 + x * 8
                    lanes = slice(t * 128, (t + 1) * 128)
                    placed = ACC[pl.ds(top, 8), lanes] + ACC[pl.ds(192 + top, 8), lanes]
                    now = U[n + 1, c, x + 1, lo, :]
                    later = (
                        2.0 * now
                        - U[n, c, x + 1, lo, :]
                        + WM[x, lo, :] * (placed - 0.25 * inside)
                    )
                    U[n + 2, c, x + 1, lo, :] = later
                    if t == 0:
                        V[n + 1, c, pl.ds(8 + x, 1), :] = later[0:1, :]
                    else:
                        YH[n + 1, c, pl.ds(x, 1), :] = later[7:8, :]
            return inner

        lax.fori_loop(0, EX, update, 0, unroll=EX)

        @pl.when(n < STEPS - 1)
        def _():
            pack_corners(n + 1)
            where_true(halo(n + 1), leaves, lambda copy: copy.start())

        @pl.when(n < STEPS - 3)
        def _():
            send_forces(n + 3)

        where_true(copies, leaves, lambda copy: copy.wait_send())
        return carry

    lax.fori_loop(0, STEPS, step, 0)
    outs[0].start()
    for out in outs:
        out.wait()


def per_device(nx, ny, *args):
    any_space = pl.BlockSpec(memory_space=pl.ANY)
    smem = pl.BlockSpec(memory_space=pltpu.SMEM)
    vmem = pltpu.VMEM
    dma = pltpu.SemaphoreType.DMA
    scratch = [
        vmem((STEPS + 2, 3, EX + 2, EY + 8, NZ), F32),
        vmem((STEPS + 1, 3, 24, NZ), F32),
        vmem((STEPS, 3, 24, NZ), F32),
        vmem((STEPS + 1, 3, 8, NZ), F32),
        vmem((STEPS, 3, 8, NZ), F32),
        vmem((STEPS, 4, 3, 1, NZ), F32),
        vmem((STEPS, 4, 3, 1, NZ), F32),
        vmem((6 * SURF + 1, EX + 1, EY, NZ), F32),
        vmem((6 * SURF + 1, EX, NZ), F32),
        vmem((6 * SURF + 1, 16, NZ), F32),
        vmem((6 * SURF + 1, 1, NZ), F32),
        vmem((6 * SURF + 1, 1, NZ), F32),
        vmem((1 + 2 * SURF, EX + 1, EY, NZ), F32),
        vmem((1 + 2 * SURF, 16, NZ), F32),
        vmem((6, EX + 1, EY + 8, NZ), F32),
        vmem((STEPS, nx, 1, 3 * PIECE), F32),
        vmem((STEPS, nx, 1, 3 * PIECE), F32),
        vmem((nx, 64, PIECE), BF16),
        vmem((256, nx * PIECE), BF16),
        vmem((384, nx * PIECE), BF16),
        vmem((384, 256), F32),
        vmem((EX, EY, NZ), F32),
        vmem((21, nx, PIECE), F32),
        vmem((nx, 2, PIECE), F32),
        vmem((2, nx, PIECE), F32),
        vmem((1, nx * PIECE), jnp.int32),
        vmem((3, EX, EY, NZ), F32),
        vmem((EX, EY, NZ), F32),
        vmem((EX, EY, NZ), jnp.int32),
        dma((8,)),
        dma((4,)),
        dma((STEPS,)),
        dma((STEPS,)),
        dma((STEPS, 8)),
        dma((STEPS, 8)),
        dma((3,)),
        dma((3,)),
    ]
    return pl.pallas_call(
        functools.partial(kernel, nx, ny),
        out_shape=(
            pltpu.VMEM((3, EX, EY, NZ), F32),
            pltpu.VMEM((6 * SURF, EX, EY, NZ), F32),
        ),
        in_specs=[any_space] * 5 + [smem] * 2 + [any_space] * 3,
        out_specs=(any_space, any_space),
        scratch_shapes=scratch,
        compiler_params=pltpu.CompilerParams(
            collective_id=0, has_side_effects=True, vmem_limit_bytes=60 * 1024 * 1024
        ),
        name="box_steps",
    )(*args[:7], jnp.transpose(args[7], (1, 0, 2)), *args[8:])


def solution(mesh):
    return jax.shard_map(
        functools.partial(per_device, mesh.shape["gx"], mesh.shape["gy"]),
        mesh=mesh,
        in_specs=(
            P(None, "gx", "gy", None),
            P(None, "gx", "gy", None),
            P(None, "gx", "gy", None),
            P("gx", "gy", None),
            P("gx", "gy", None),
            P(),
            P(),
            P("gx", None, "gy"),
            P("gx", None, "gy"),
            P("gx", "gy"),
        ),
        out_specs=(P(None, "gx", "gy", None), P(None, "gx", "gy", None)),
        check_vma=False,
    )
```
